256 devices in a mesh: gx: 16 (over y, z_hi), gy: 16 (over z_lo, x, core).
Axes of the slice: x: 4, y: 4, z: 8 (z_hi: 4, z_lo: 2; z = z_hi * 2 + z_lo), core: 2. Of those that a mesh axis runs over, the one named last changes fastest.
Arguments:
- density: bfloat16 [32, 64, 32, 128], P(None, 'gx', 'gy'), may hold values from -12 to 12
- weight_one: bfloat16 [32, 864], replicated, may hold values from -0.21875 to 0.21875
- weight_two: bfloat16 [128, 864], replicated, may hold values from -0.21875 to 0.21875
- cotangent: bfloat16 [128, 64, 32, 128], P(None, 'gx', 'gy'), may hold values from -6 to 6
Outputs:
- update_one: float32 [32, 864], replicated
- update_two: float32 [128, 864], replicated
The draws below stay inside these ranges and needn't reach their ends.
All inputs are finite; a program needn't handle non-finite values. Where the reference program divides by a largest or mean magnitude, that divisor is 1e-20 or more.
Results may differ from the reference program's by a relative error of at most 0.0033.
Values may be sent and summed in bfloat16 or wider, within the bound.
No kernel may reach another device: no remote copies, remote signals or barrier semaphores. Data moves between devices by JAX's collectives and lax.ppermute only.
A program may use at most 128 MiB of HBM per device.

```python
import math
import jax
import jax.numpy as jnp
from jax import lax

CH = 32
COUT = 128
CZ = 128
ITERS = 3
PATCH = 864
NX = 64
NY = 32


def draw_density(key, part):
    key = jax.random.fold_in(key, 11)
    scale_key, value_key = jax.random.split(key)
    scales = jnp.exp(jax.random.uniform(scale_key, (CH, 1, 1, 1), jnp.float32, math.log(0.3), math.log(3.0)))
    values = jnp.clip(jax.random.normal(value_key, (CH, NX, NY, CZ), jnp.float32), -4.0, 4.0)
    return (values * scales).astype(jnp.bfloat16)


def levels(key, extent, cuts, least, largest):
    def one(dim, blocks):
        heights = jax.random.uniform(jax.random.fold_in(jax.random.fold_in(key, 6), dim), (blocks,), jnp.float32, least / len(cuts), largest / len(cuts))
        return jnp.repeat(jnp.exp(heights), extent[dim] // blocks).reshape((-1,) + (1,) * (len(extent) - dim - 1))

    loudness = one(*cuts[0])
    for cut in cuts[1:]:
        loudness = loudness * one(*cut)
    return loudness


def normal_values(key, extent, width, reach, cuts=(), held_as=jnp.bfloat16):
    result = width * jax.random.normal(key, extent, jnp.float32)
    if cuts:
        result = result * levels(key, extent, cuts, -0.22, 0.18)
    return jnp.clip(result, -reach, reach).astype(held_as)


def setup_inputs(seed: int = 0) -> dict:
    key_list = jax.random.split(jax.random.key(seed), 5)
    return {
        "density": draw_density(jax.random.fold_in(key_list[4], 71), 0),
        "weight_one": normal_values(key_list[1], (CH, PATCH), PATCH ** -0.5, 0.21875),
        "weight_two": normal_values(key_list[2], (COUT, PATCH), PATCH ** -0.5, 0.21875),
        "cotangent": normal_values(key_list[3], (COUT, NX, NY, CZ), 1.0, 6.0, ((1, 16), (2, 16))),
    }


damping = 0.1
highest = lax.Precision.HIGHEST

def depth_pad(volume):
    return jnp.pad(volume, ((0, 0), (0, 0), (0, 0), (1, 1)))

def wrap_pad(volume):
    return jnp.pad(volume, ((0, 0), (1, 1), (1, 1), (0, 0)), mode='wrap')

def plane_patches(padded, plane_index):
    channels = padded.shape[0]
    span_y = padded.shape[2] - 2
    span_z = padded.shape[3] - 2
    window = lax.dynamic_slice_in_dim(padded, plane_index, 3, 1)
    pieces = []
    for offset in range(27):
        along_x = offset // 9
        along_y = offset // 3 % 3
        along_z = offset % 3
        pieces.append(window[:, along_x, along_y:along_y + span_y, along_z:along_z + span_z])
    return jnp.stack(pieces, axis=1).reshape(channels * 27, span_y * span_z)

def outer_sum(left, right):
    return lax.dot_general(left, right, (((1,), (1,)), ((), ())), preferred_element_type=jnp.float32)

def silu_slope(values):
    logistic = jax.nn.sigmoid(values)
    return logistic * (1.0 + values * (1.0 - logistic))

def transpose_conv(cot_padded, weight_two, span_x, span_y, span_z):
    outputs = weight_two.shape[0]
    channels = weight_two.shape[1] // 27
    kernel = weight_two.reshape(outputs, channels, 27)
    summed = jnp.zeros((channels, span_x * span_y * span_z), jnp.float32)
    for offset in range(27):
        along_x = offset // 9
        along_y = offset // 3 % 3
        along_z = offset % 3
        window = cot_padded[:, 2 - along_x:2 - along_x + span_x, 2 - along_y:2 - along_y + span_y, 2 - along_z:2 - along_z + span_z]
        summed = summed + jnp.dot(kernel[:, :, offset].T, window.reshape(outputs, -1), preferred_element_type=jnp.float32)
    return summed

def inverse_root(matrix):
    matrix_order = matrix.shape[0]
    row_bound = jnp.max(lax.optimization_barrier(jnp.sum(jnp.abs(matrix), axis=1)))
    scaled = matrix / row_bound
    identity = jnp.eye(matrix_order, dtype=jnp.float32)
    iterate = (3.0 * identity - scaled) / 2.0
    for step_index in range(ITERS - 1):
        product = jnp.dot(iterate, scaled, precision=highest)
        product = jnp.dot(product, iterate, precision=highest)
        product = jnp.dot(product, iterate, precision=highest)
        iterate = (3.0 * iterate - product) / 2.0
    return iterate / jnp.sqrt(row_bound)

def reference(density, weight_one, weight_two, cotangent):
    channels, span_x, span_y, span_z = density.shape
    outputs = cotangent.shape[0]
    patch_size = channels * 27
    total_cells = span_x * span_y * span_z
    density_pad = depth_pad(wrap_pad(density))
    back_grad = transpose_conv(depth_pad(wrap_pad(cotangent)), weight_two, span_x, span_y, span_z)
    back_grad = back_grad.reshape(channels, span_x, span_y * span_z)

    def first_pass(totals, plane_index):
        columns = plane_patches(density_pad, plane_index)
        linear = jnp.dot(weight_one, columns, preferred_element_type=jnp.float32)
        upstream = lax.dynamic_index_in_dim(back_grad, plane_index, 1, keepdims=False)
        signal = (upstream * silu_slope(linear)).astype(jnp.bfloat16)
        updated = (totals[0] + outer_sum(columns, columns), totals[1] + outer_sum(signal, columns), totals[2] + outer_sum(signal, signal))
        return (updated, jax.nn.silu(linear).astype(jnp.bfloat16))
    initial = (jnp.zeros((patch_size, patch_size), jnp.float32), jnp.zeros((channels, patch_size), jnp.float32), jnp.zeros((channels, channels), jnp.float32))
    plane_ids = jnp.arange(span_x, dtype=jnp.int32)
    first_totals, hidden_planes = lax.scan(first_pass, initial, plane_ids)
    hidden = jnp.moveaxis(hidden_planes, 0, 1).reshape(channels, span_x, span_y, span_z)
    hidden_pad = depth_pad(wrap_pad(hidden))
    cot_planes = cotangent.reshape(outputs, span_x, span_y * span_z)

    def second_pass(totals, plane_index):
        columns = plane_patches(hidden_pad, plane_index)
        signal = lax.dynamic_index_in_dim(cot_planes, plane_index, 1, keepdims=False)
        return ((totals[0] + outer_sum(columns, columns), totals[1] + outer_sum(signal, columns)), plane_index)
    second_init = (jnp.zeros((patch_size, patch_size), jnp.float32), jnp.zeros((outputs, patch_size), jnp.float32))
    second_totals, unused = lax.scan(second_pass, second_init, plane_ids)
    cot_flat = cotangent.reshape(outputs, -1)
    gcov_two = outer_sum(cot_flat, cot_flat)
    eye_patch = jnp.eye(patch_size, dtype=jnp.float32)
    a_one = first_totals[0] / total_cells + damping * eye_patch
    a_two = second_totals[0] / total_cells + damping * eye_patch
    c_one = first_totals[2] / total_cells + damping * jnp.eye(channels, dtype=jnp.float32)
    c_two = gcov_two / total_cells + damping * jnp.eye(outputs, dtype=jnp.float32)
    grad_one = first_totals[1] / math.sqrt(total_cells)
    grad_two = second_totals[1] / math.sqrt(total_cells)
    update_one = jnp.dot(jnp.dot(inverse_root(c_one), grad_one, precision=highest), inverse_root(a_one), precision=highest)
    update_two = jnp.dot(jnp.dot(inverse_root(c_two), grad_two, precision=highest), inverse_root(a_two), precision=highest)
    return (update_one, update_two)
```

```python
import functools
import math

import jax
import jax.numpy as jnp
import numpy as np
from jax import lax
from jax.experimental import pallas as pl
from jax.experimental.pallas import tpu as pltpu
from jax.sharding import Mesh, PartitionSpec as P

ITERS = 3
DAMPING = 0.1
F32 = jnp.float32
BF16 = jnp.bfloat16
VMEM_LIMIT = 48 * 1024 * 1024
ROWS = 1024
LANES = 128


def dot_nt(left, right):
    return lax.dot_general(left, right, (((1,), (1,)), ((), ())), preferred_element_type=F32)


def dot_nn(left, right):
    return jnp.dot(left, right, preferred_element_type=F32)


def lane_ids(shape):
    return lax.broadcasted_iota(jnp.int32, shape, 1)


def from_below(values):
    return jnp.where(lane_ids(values.shape) == 0, 0.0, pltpu.roll(values, 1, 1))


def from_above(values):
    return jnp.where(
        lane_ids(values.shape) == LANES - 1, 0.0, pltpu.roll(values, LANES - 1, 1)
    )


def correlations(stack_ref, out_ref):
    base = stack_ref[0:96, :]
    out_ref[:, 0:864] = dot_nt(base, stack_ref[...])
    lower = stack_ref[96:288, :]
    first = dot_nt(lower, stack_ref[288:384, :])
    second = dot_nt(lower, stack_ref[576:672, :])
    out_ref[:, 864:960] = first[0:96]
    out_ref[:, 960:1056] = first[96:192]
    out_ref[:, 1056:1152] = second[0:96]
    out_ref[:, 1152:1248] = second[96:192]
    out_ref[:, 1248:1280] = jnp.zeros((96, 32), F32)


def field_kernel(
    core_ref, near_ref, mid_ref, far_ref, weight_ref,
    keep_ref, send_ref, pre_ref, stack_one_ref, stack_two_ref,
    shifted_ref, hidden_ref, acc_ref, corr_one_ref, corr_two_ref,
):
    parts = (near_ref, mid_ref, far_ref)
    for x in range(8):
        for y in range(6):
            column = parts[y // 2][x, y % 2].astype(F32)
            lanes = slice((x * 6 + y) * LANES, (x * 6 + y + 1) * LANES)
            shifted_ref[0:32, lanes] = from_below(column).astype(BF16)
            shifted_ref[32:64, lanes] = column.astype(BF16)
            shifted_ref[64:96, lanes] = from_above(column).astype(BF16)
    weight = weight_ref[...]
    acc_ref[...] = jnp.zeros_like(acc_ref)
    for x in range(8):
        terms = dot_nn(weight, shifted_ref[:, x * 768 : (x + 1) * 768])
        for a in range(3):
            row = x - a + 1
            if 1 <= row <= 6:
                total = acc_ref[row - 1]
                for b in range(3):
                    first = (3 * a + b) * 32
                    total = total + terms[first : first + 32, b * LANES : b * LANES + 512]
                acc_ref[row - 1] = total
    for row in range(6):
        linear = acc_ref[row]
        if row < 4:
            pre_ref[row] = linear[:, 0:256]
        hidden = (linear / (1.0 + jnp.exp(-linear))).astype(BF16).astype(F32)
        for y in range(4):
            column = hidden[:, y * LANES : (y + 1) * LANES]
            lanes = slice((row * 4 + y) * LANES, (row * 4 + y + 1) * LANES)
            hidden_ref[0:32, lanes] = from_below(column).astype(BF16)
            hidden_ref[32:64, lanes] = column.astype(BF16)
            hidden_ref[64:96, lanes] = from_above(column).astype(BF16)
    for a in range(3):
        for b in range(3):
            rows = slice((3 * a + b) * 96, (3 * a + b + 1) * 96)
            for x in range(4):
                lanes = slice(x * 256, (x + 1) * 256)
                one = ((x + a) * 6 + b) * LANES
                two = ((x + a) * 4 + b) * LANES
                stack_one_ref[rows, lanes] = shifted_ref[:, one : one + 256]
                stack_two_ref[rows, lanes] = hidden_ref[:, two : two + 256]
    correlations(stack_one_ref, corr_one_ref)
    correlations(stack_two_ref, corr_two_ref)
    is_first = core_ref[0] == 0
    for tile in range(10):
        lanes = slice(tile * LANES, (tile + 1) * LANES)
        rows = slice(tile * 96, (tile + 1) * 96)
        one = corr_one_ref[:, lanes]
        two = corr_two_ref[:, lanes]
        keep_ref[rows, :] = jnp.where(is_first, one, two)
        send_ref[rows, :] = jnp.where(is_first, two, one)
    keep_ref[960:ROWS, :] = jnp.zeros((ROWS - 960, LANES), F32)
    send_ref[960:ROWS, :] = jnp.zeros((ROWS - 960, LANES), F32)


def gradient_kernel(
    core_ref, near_ref, mid_ref, weight_ref, pre_ref, stack_one_ref, stack_two_ref,
    keep_ref, send_ref,
    acc_ref, signal_ref, cells_ref, one_ref, two_ref,
):
    weight = weight_ref[...]
    acc_ref[...] = jnp.zeros_like(acc_ref)
    for x in range(6):
        row_cells = jnp.concatenate(
            [near_ref[x, 0], near_ref[x, 1], mid_ref[x, 0], mid_ref[x, 1]], axis=1
        )
        terms = dot_nn(weight, row_cells)
        for a in range(3):
            row = x + a - 1
            if 1 <= row <= 4:
                for e in range(3):
                    total = acc_ref[e, row - 1]
                    for b in range(3):
                        first = (9 * e + 3 * a + b) * 32
                        total = total + terms[
                            first : first + 32, (2 - b) * LANES : (4 - b) * LANES
                        ]
                    acc_ref[e, row - 1] = total
    for row in range(4):
        linear = pre_ref[row]
        logistic = 1.0 / (1.0 + jnp.exp(-linear))
        slope = logistic * (1.0 + linear * (1.0 - logistic))
        for y in range(2):
            lanes = slice(y * LANES, (y + 1) * LANES)
            back = (
                from_above(acc_ref[0, row][:, lanes])
                + acc_ref[1, row][:, lanes]
                + from_below(acc_ref[2, row][:, lanes])
            )
            place = slice((row * 2 + y) * LANES, (row * 2 + y + 1) * LANES)
            signal_ref[:, place] = (back * slope[:, lanes]).astype(BF16)
            cells_ref[:, place] = mid_ref[row + 2, y]
    signal = signal_ref[...]
    cells = cells_ref[...]
    one_ref[...] = jnp.zeros_like(one_ref)
    one_ref[0:32, 0:864] = dot_nt(signal, stack_one_ref[...])
    one_ref[0:32, 896:928] = dot_nt(signal, signal)
    two_ref[:, 0:864] = dot_nt(cells, stack_two_ref[...])
    two_ref[:, 864:896] = jnp.zeros((128, 32), F32)
    two_ref[:, 896:1024] = dot_nt(cells, cells)
    is_first = core_ref[0] == 0
    for tile in range(8):
        lanes = slice(tile * LANES, (tile + 1) * LANES)
        rows = slice(tile * 128, (tile + 1) * 128)
        one = one_ref[:, lanes]
        two = two_ref[:, lanes]
        keep_ref[rows, :] = jnp.where(is_first, one, two)
        send_ref[rows, :] = jnp.where(is_first, two, one)


def split_rows(values):
    high = values.astype(BF16)
    low = (values - high.astype(F32)).astype(BF16)
    return jnp.concatenate([high, low], axis=0)


def root_kernel(total_cells, sums_ref, order_ref, out_ref, strip_ref, full_ref, factor_ref):
    count, triple, _ = sums_ref.shape
    values = sums_ref[...].astype(F32).reshape(count, 3, triple // 3, LANES)
    corr = values[:, 0].reshape(ROWS, LANES)
    grads = (values[:, 1] + values[:, 2]).reshape(ROWS, LANES)
    corr = jnp.concatenate([corr[96 * j : 96 * j + 96] for j in range(10)], axis=1)
    gradient = jnp.concatenate([grads[128 * j : 128 * j + 128] for j in range(7)], axis=1)[:, 0:864]

    def identity(order, dtype):
        rows = lax.broadcasted_iota(jnp.int32, (order, order), 0)
        return jnp.where(rows == lane_ids((order, order)), 1.0, 0.0).astype(dtype)

    eye_96 = identity(96, BF16)
    eye_288 = identity(288, BF16)
    strip_ref[0, :, 0:96] = dot_nt(eye_96, corr[:, 192:288].astype(BF16))
    strip_ref[0, :, 96:192] = dot_nt(eye_96, corr[:, 96:192].astype(BF16))
    strip_ref[0, :, 192:480] = corr[:, 0:288]
    strip_ref[1, :, 0:96] = corr[:, 960:1056]
    strip_ref[1, :, 96:192] = corr[:, 864:960]
    strip_ref[1, :, 192:480] = corr[:, 288:576]
    strip_ref[2, :, 0:96] = corr[:, 1152:1248]
    strip_ref[2, :, 96:192] = corr[:, 1056:1152]
    strip_ref[2, :, 192:480] = corr[:, 576:864]
    for b in range(3):
        for step in range(3):
            piece = strip_ref[step, :, (2 - b) * 96 : (2 - b) * 96 + 288]
            for a in range(3 - step):
                first = a * 288 + b * 96
                full_ref[first : first + 96, (a + step) * 288 : (a + step + 1) * 288] = piece
    turned_one = dot_nt(eye_288, full_ref[0:288, 288:576].astype(BF16))
    turned_two = dot_nt(eye_288, full_ref[0:288, 576:864].astype(BF16))
    full_ref[288:576, 0:288] = turned_one
    full_ref[576:864, 288:576] = turned_one
    full_ref[576:864, 0:288] = turned_two
    whole = full_ref[...]
    factor_ref[...] = whole.astype(BF16)
    bound = jnp.max(jnp.sum(jnp.abs(whole), axis=0, keepdims=True)) / total_cells + DAMPING
    scale = 1.0 / (bound * total_cells)
    shift = DAMPING / bound

    def times(rows):
        product = dot_nn(split_rows(rows), factor_ref[...])
        return (product[0:128] + product[128:256]) * scale + rows * shift

    def once(rows):
        return 1.5 * rows - 0.5 * times(rows)

    def iterate(rows, step):
        if step == 0:
            return once(rows)
        first = iterate(rows, step - 1)
        second = iterate(iterate(times(first), step - 1), step - 1)
        return 1.5 * first - 0.5 * second

    right = iterate(gradient, ITERS - 1)

    eye_128 = identity(128, F32)
    small = grads[896:1024] / total_cells + DAMPING * eye_128
    small_bound = jnp.max(jnp.sum(jnp.abs(small), axis=0, keepdims=True))
    scaled = small / small_bound
    root = 1.5 * eye_128 - 0.5 * scaled
    exact = functools.partial(
        jnp.dot, precision=lax.Precision.HIGHEST, preferred_element_type=F32
    )
    for _ in range(ITERS - 1):
        product = exact(exact(exact(root, scaled), root), root)
        root = 1.5 * root - 0.5 * product
    factor = 1.0 / (math.sqrt(total_cells) * jnp.sqrt(small_bound) * jnp.sqrt(bound))
    update = exact(root, right) * factor
    ordered = dot_nn(split_rows(update), order_ref[...])
    out_ref[...] = ordered[0:128] + ordered[128:256]


def plane_order():
    order = np.zeros((864, 864), np.float32)
    for offset in range(27):
        for channel in range(32):
            order[offset * 32 + channel, channel * 27 + offset] = 1.0
    return jnp.asarray(order, BF16)


def params():
    return pltpu.CompilerParams(vmem_limit_bytes=VMEM_LIMIT)


def in_vmem(count):
    return [pl.BlockSpec(memory_space=pltpu.VMEM)] * count


def field_sums(core, near, mid, far, weight):
    shape = jax.ShapeDtypeStruct
    return pl.pallas_call(
        field_kernel,
        out_shape=(
            shape((ROWS, LANES), F32),
            shape((ROWS, LANES), F32),
            shape((4, 32, 256), F32),
            shape((864, 1024), BF16),
            shape((864, 1024), BF16),
        ),
        in_specs=[pl.BlockSpec(memory_space=pltpu.SMEM)] + in_vmem(4),
        out_specs=tuple(in_vmem(5)),
        scratch_shapes=[
            pltpu.VMEM((96, 6144), BF16),
            pltpu.VMEM((96, 3072), BF16),
            pltpu.VMEM((6, 32, 512), F32),
            pltpu.VMEM((96, 1280), F32),
            pltpu.VMEM((96, 1280), F32),
        ],
        compiler_params=params(),
        cost_estimate=pl.CostEstimate(
            flops=2_000_000_000, bytes_accessed=6_000_000, transcendentals=200_000
        ),
        name="field_sums",
    )(core, near, mid, far, weight)


def gradient_sums(core, near, mid, weight, pre, stack_one, stack_two):
    shape = jax.ShapeDtypeStruct
    return pl.pallas_call(
        gradient_kernel,
        out_shape=(shape((ROWS, LANES), F32), shape((ROWS, LANES), F32)),
        in_specs=[pl.BlockSpec(memory_space=pltpu.SMEM)] + in_vmem(6),
        out_specs=tuple(in_vmem(2)),
        scratch_shapes=[
            pltpu.VMEM((3, 4, 32, 256), F32),
            pltpu.VMEM((32, 1024), BF16),
            pltpu.VMEM((128, 1024), BF16),
            pltpu.VMEM((128, 1024), F32),
            pltpu.VMEM((128, 1024), F32),
        ],
        compiler_params=params(),
        cost_estimate=pl.CostEstimate(
            flops=2_000_000_000, bytes_accessed=6_000_000, transcendentals=200_000
        ),
        name="gradient_sums",
    )(core, near, mid, weight, pre, stack_one, stack_two)


def updates(total_cells, sums, order):
    return pl.pallas_call(
        functools.partial(root_kernel, total_cells),
        out_shape=jax.ShapeDtypeStruct((128, 864), F32),
        in_specs=in_vmem(2),
        out_specs=in_vmem(1)[0],
        scratch_shapes=[
            pltpu.VMEM((3, 96, 512), F32),
            pltpu.VMEM((864, 864), F32),
            pltpu.VMEM((864, 864), BF16),
        ],
        compiler_params=params(),
        cost_estimate=pl.CostEstimate(
            flops=8_000_000_000, bytes_accessed=6_000_000, transcendentals=1000
        ),
        name="updates",
    )(sums, order)


def on_device(density, weight_one, weight_two, cotangent):
    grid_x = lax.axis_size("gx")
    grid_y = lax.axis_size("gc") * lax.axis_size("core")
    total_cells = 1024 * grid_x * grid_y
    core = lax.axis_index("core").astype(jnp.int32).reshape(1)

    def next_x(block):
        return lax.ppermute(block, "gx", [((i + 1) % grid_x, i) for i in range(grid_x)])

    def next_y(block, distance):
        pairs = [((i + distance) % grid_y, i) for i in range(grid_y)]
        return lax.ppermute(block, ("gc", "core"), pairs)

    def other_core(block):
        return lax.ppermute(block, "core", [(0, 1), (1, 0)])

    field = density.transpose(1, 2, 0, 3)
    cells = cotangent.transpose(1, 2, 0, 3)
    field = jnp.concatenate([field, next_x(field)], axis=0)
    cells = jnp.concatenate([cells, next_x(cells[0:2])], axis=0)
    field_mid = next_y(field, 1)
    field_far = next_y(field, 2)
    cells_mid = next_y(cells, 1)
    kernel_one = weight_one.reshape(32, 32, 3, 3, 3).transpose(2, 3, 0, 4, 1).reshape(288, 96)
    kernel_two = weight_two.reshape(128, 32, 3, 3, 3).transpose(4, 2, 3, 1, 0).reshape(864, 128)
    keep_corr, send_corr, pre, stack_one, stack_two = field_sums(
        core, field, field_mid, field_far, kernel_one
    )
    keep_grad, send_grad = gradient_sums(
        core, cells, cells_mid, kernel_two, pre, stack_one, stack_two
    )
    corr = keep_corr + other_core(send_corr)
    grad = keep_grad + other_core(send_grad)
    group = grid_x * lax.axis_size("gc")
    chunk = ROWS // group

    def packed(corr, grad):
        high = lax.reduce_precision(grad, 8, 7)
        pieces = (corr.astype(BF16), high.astype(BF16), (grad - high).astype(BF16))
        return jnp.concatenate(
            [piece.reshape(-1, chunk, LANES) for piece in pieces], axis=1
        )

    parts = packed(corr, grad)
    parts = lax.all_to_all(parts, ("gx", "gc"), 0, 0, tiled=True)
    summed = jnp.sum(parts.astype(F32), axis=0)
    own = packed(summed[0:chunk], summed[chunk : 2 * chunk] + summed[2 * chunk : 3 * chunk])
    copies = jnp.broadcast_to(own, (group, 3 * chunk, LANES))
    gathered = lax.all_to_all(copies, ("gx", "gc"), 0, 0, tiled=True)
    mine = updates(float(total_cells), gathered, plane_order())
    other = other_core(mine)
    is_first = core[0] == 0
    update_one = jnp.where(is_first, mine[0:32], other[0:32])
    update_two = jnp.where(is_first, other, mine)
    return (update_one, update_two)


def solution(mesh):
    grid_x, grid_y = mesh.shape["gx"], mesh.shape["gy"]
    inner = Mesh(mesh.devices.reshape(grid_x, grid_y // 2, 2), ("gx", "gc", "core"))
    split = P(None, "gx", ("gc", "core"), None)
    return jax.shard_map(
        on_device,
        mesh=inner,
        in_specs=(split, P(), P(), split),
        out_specs=(P(), P()),
        check_vma=False,
    )
```

```python
import functools
import math

import jax
import jax.numpy as jnp
import numpy as np
from jax import lax
from jax.experimental import pallas as pl
from jax.experimental.pallas import tpu as pltpu
from jax.sharding import Mesh, PartitionSpec as P

ITERS = 3
DAMPING = 0.1
F32 = jnp.float32
BF16 = jnp.bfloat16
VMEM_LIMIT = 20 * 1024 * 1024
ROWS = 1024
LANES = 128


def dot_nt(left, right):
    return lax.dot_general(left, right, (((1,), (1,)), ((), ())), preferred_element_type=F32)


def dot_nn(left, right):
    return jnp.dot(left, right, preferred_element_type=F32)


def lane_ids(shape):
    return lax.broadcasted_iota(jnp.int32, shape, 1)


def from_below(values):
    return jnp.where(lane_ids(values.shape) == 0, 0.0, pltpu.roll(values, 1, 1))


def from_above(values):
    return jnp.where(
        lane_ids(values.shape) == LANES - 1, 0.0, pltpu.roll(values, LANES - 1, 1)
    )


def contribution_kernel(cells_ref, weight_ref, rest_ref, send_ref, square_ref, acc_ref, flat_ref):
    weight = weight_ref[...]
    acc_ref[...] = jnp.zeros_like(acc_ref)
    for x in range(4):
        for y in range(2):
            place = slice((x * 2 + y) * LANES, (x * 2 + y + 1) * LANES)
            flat_ref[:, place] = cells_ref[x, y]
        terms = dot_nn(weight, flat_ref[:, x * 256 : (x + 1) * 256])
        for e in range(3):
            for a in range(3):
                for b in range(3):
                    first = (9 * e + 3 * a + b) * 32
                    lanes = slice(b * LANES, (b + 2) * LANES)
                    acc_ref[e, x + a, :, lanes] = (
                        acc_ref[e, x + a, :, lanes] + terms[first : first + 32]
                    )
    for row in range(6):
        for y in range(4):
            lanes = slice(y * LANES, (y + 1) * LANES)
            total = (
                from_above(acc_ref[0, row, :, lanes])
                + acc_ref[1, row, :, lanes]
                + from_below(acc_ref[2, row, :, lanes])
            )
            if y < 2:
                rest_ref[row, y] = total
            else:
                send_ref[row, y - 2] = total
    cells = flat_ref[...]
    square_ref[...] = dot_nt(cells, cells)


def stacked_products(left_ref, stack_ref, out_ref):
    out_ref[:, 0:864] = dot_nt(left_ref[...], stack_ref[...])
    lower = stack_ref[96:288, :]
    first = dot_nt(lower, stack_ref[288:384, :])
    second = dot_nt(lower, stack_ref[576:672, :])
    out_ref[0:96, 864:960] = first[0:96]
    out_ref[0:96, 960:1056] = first[96:192]
    out_ref[0:96, 1056:1152] = second[0:96]
    out_ref[0:96, 1152:1248] = second[96:192]
    out_ref[0:96, 1248:1280] = jnp.zeros((96, 32), F32)


def sums_kernel(
    core_ref, left_ref, own_ref, right_ref, back_ref, corner_ref, cells_ref, square_ref, weight_ref,
    keep_ref, send_ref,
    shifted_ref, hidden_ref, acc_ref, stack_one_ref, stack_two_ref,
    rows_one_ref, rows_two_ref, out_one_ref, out_two_ref,
):
    parts = (left_ref, own_ref, right_ref)
    for x in range(8):
        for y in range(6):
            column = parts[y // 2][x, y % 2].astype(F32)
            lanes = slice((x * 6 + y) * LANES, (x * 6 + y + 1) * LANES)
            shifted_ref[0:32, lanes] = from_below(column).astype(BF16)
            shifted_ref[32:64, lanes] = column.astype(BF16)
            shifted_ref[64:96, lanes] = from_above(column).astype(BF16)
    weight = weight_ref[...]
    acc_ref[...] = jnp.zeros_like(acc_ref)
    for x in range(8):
        terms = dot_nn(weight, shifted_ref[:, x * 768 : (x + 1) * 768])
        for a in range(3):
            row = x - a + 1
            if 1 <= row <= 6:
                total = acc_ref[row - 1]
                for b in range(3):
                    first = (3 * a + b) * 32
                    total = total + terms[first : first + 32, b * LANES : b * LANES + 512]
                acc_ref[row - 1] = total
    for row in range(6):
        linear = acc_ref[row]
        logistic = 1.0 / (1.0 + jnp.exp(-linear))
        hidden = (linear * logistic).astype(BF16).astype(F32)
        for y in range(4):
            column = hidden[:, y * LANES : (y + 1) * LANES]
            lanes = slice((row * 4 + y) * LANES, (row * 4 + y + 1) * LANES)
            hidden_ref[0:32, lanes] = from_below(column).astype(BF16)
            hidden_ref[32:64, lanes] = column.astype(BF16)
            hidden_ref[64:96, lanes] = from_above(column).astype(BF16)
        if row < 4:
            slope = logistic * (1.0 + linear * (1.0 - logistic))
            for y in range(2):
                back = back_ref[row, y]
                if row < 2:
                    back = back + corner_ref[row, y]
                place = slice((row * 2 + y) * LANES, (row * 2 + y + 1) * LANES)
                signal = back * slope[:, y * LANES : (y + 1) * LANES]
                rows_one_ref[96:128, place] = signal.astype(BF16)
                rows_two_ref[96:224, place] = cells_ref[row, y]
    for a in range(3):
        for b in range(3):
            rows = slice((3 * a + b) * 96, (3 * a + b + 1) * 96)
            for x in range(4):
                lanes = slice(x * 256, (x + 1) * 256)
                one = ((x + a) * 6 + b) * LANES
                two = ((x + a) * 4 + b) * LANES
                stack_one_ref[rows, lanes] = shifted_ref[:, one : one + 256]
                stack_two_ref[rows, lanes] = hidden_ref[:, two : two + 256]
    rows_one_ref[0:96, :] = stack_one_ref[0:96, :]
    rows_two_ref[0:96, :] = stack_two_ref[0:96, :]
    stacked_products(rows_one_ref, stack_one_ref, out_one_ref)
    stacked_products(rows_two_ref, stack_two_ref, out_two_ref)
    signal = rows_one_ref[96:128, :]
    square_one = dot_nt(signal, signal)
    is_first = core_ref[0] == 0

    def put(rows, one, two):
        keep_ref[rows, :] = jnp.where(is_first, one, two)
        send_ref[rows, :] = jnp.where(is_first, two, one)

    for tile in range(10):
        lanes = slice(tile * LANES, (tile + 1) * LANES)
        put(
            slice(tile * 96, (tile + 1) * 96), out_one_ref[0:96, lanes], out_two_ref[0:96, lanes]
        )
    nothing = jnp.zeros((96, LANES), F32)
    keep_ref[960:ROWS, :] = nothing[0 : ROWS - 960]
    send_ref[960:ROWS, :] = nothing[0 : ROWS - 960]
    for tile in range(7):
        lanes = slice(tile * LANES, (tile + 1) * LANES)
        one = out_one_ref[96:128, lanes]
        two = out_two_ref[96:224, lanes]
        if tile == 6:
            one = jnp.where(lane_ids(one.shape) < 96, one, 0.0)
            two = jnp.where(lane_ids(two.shape) < 96, two, 0.0)
        put(
            slice(ROWS + tile * 128, ROWS + (tile + 1) * 128),
            jnp.concatenate([one, nothing], axis=0),
            two,
        )
    wide = jnp.concatenate([square_one, jnp.zeros((32, 96), F32)], axis=1)
    put(
        slice(ROWS + 896, ROWS + 1024), jnp.concatenate([wide, nothing], axis=0), square_ref[...]
    )


def split_rows(values):
    high = values.astype(BF16)
    low = (values - high.astype(F32)).astype(BF16)
    return jnp.concatenate([high, low], axis=0)


def root_kernel(total_cells, sums_ref, order_ref, out_ref, strip_ref, full_ref, factor_ref):
    count, triple, _ = sums_ref.shape
    values = sums_ref[...].astype(F32).reshape(count, 3, triple // 3, LANES)
    corr = values[:, 0].reshape(ROWS, LANES)
    grads = (values[:, 1] + values[:, 2]).reshape(ROWS, LANES)
    corr = jnp.concatenate([corr[96 * j : 96 * j + 96] for j in range(10)], axis=1)
    gradient = jnp.concatenate([grads[128 * j : 128 * j + 128] for j in range(7)], axis=1)[:, 0:864]

    def identity(order, dtype):
        rows = lax.broadcasted_iota(jnp.int32, (order, order), 0)
        return jnp.where(rows == lane_ids((order, order)), 1.0, 0.0).astype(dtype)

    eye_96 = identity(96, BF16)
    eye_288 = identity(288, BF16)
    strip_ref[0, :, 0:96] = dot_nt(eye_96, corr[:, 192:288].astype(BF16))
    strip_ref[0, :, 96:192] = dot_nt(eye_96, corr[:, 96:192].astype(BF16))
    strip_ref[0, :, 192:480] = corr[:, 0:288]
    strip_ref[1, :, 0:96] = corr[:, 960:1056]
    strip_ref[1, :, 96:192] = corr[:, 864:960]
    strip_ref[1, :, 192:480] = corr[:, 288:576]
    strip_ref[2, :, 0:96] = corr[:, 1152:1248]
    strip_ref[2, :, 96:192] = corr[:, 1056:1152]
    strip_ref[2, :, 192:480] = corr[:, 576:864]
    for b in range(3):
        for step in range(3):
            piece = strip_ref[step, :, (2 - b) * 96 : (2 - b) * 96 + 288]
            for a in range(3 - step):
                first = a * 288 + b * 96
                full_ref[first : first + 96, (a + step) * 288 : (a + step + 1) * 288] = piece
    turned_one = dot_nt(eye_288, full_ref[0:288, 288:576].astype(BF16))
    turned_two = dot_nt(eye_288, full_ref[0:288, 576:864].astype(BF16))
    full_ref[288:576, 0:288] = turned_one
    full_ref[576:864, 288:576] = turned_one
    full_ref[576:864, 0:288] = turned_two
    whole = full_ref[...]
    factor_ref[...] = whole.astype(BF16)
    bound = jnp.max(jnp.sum(jnp.abs(whole), axis=0, keepdims=True)) / total_cells + DAMPING
    scale = 1.0 / (bound * total_cells)
    shift = DAMPING / bound

    def times(rows):
        product = dot_nn(split_rows(rows), factor_ref[...])
        return (product[0:128] + product[128:256]) * scale + rows * shift

    def once(rows):
        return 1.5 * rows - 0.5 * times(rows)

    def iterate(rows, step):
        if step == 0:
            return once(rows)
        first = iterate(rows, step - 1)
        second = iterate(iterate(times(first), step - 1), step - 1)
        return 1.5 * first - 0.5 * second

    right = iterate(gradient, ITERS - 1)

    eye_128 = identity(128, F32)
    small = grads[896:1024] / total_cells + DAMPING * eye_128
    small_bound = jnp.max(jnp.sum(jnp.abs(small), axis=0, keepdims=True))
    scaled = small / small_bound
    root = 1.5 * eye_128 - 0.5 * scaled
    exact = functools.partial(
        jnp.dot, precision=lax.Precision.HIGHEST, preferred_element_type=F32
    )
    for _ in range(ITERS - 1):
        product = exact(exact(exact(root, scaled), root), root)
        root = 1.5 * root - 0.5 * product
    factor = 1.0 / (math.sqrt(total_cells) * jnp.sqrt(small_bound) * jnp.sqrt(bound))
    update = exact(root, right) * factor
    ordered = dot_nn(split_rows(update), order_ref[...])
    out_ref[...] = ordered[0:128] + ordered[128:256]


def plane_order():
    order = np.zeros((864, 864), np.float32)
    for offset in range(27):
        for channel in range(32):
            order[offset * 32 + channel, channel * 27 + offset] = 1.0
    return jnp.asarray(order, BF16)


def params():
    return pltpu.CompilerParams(vmem_limit_bytes=VMEM_LIMIT)


def in_vmem(count):
    return [pl.BlockSpec(memory_space=pltpu.VMEM)] * count


def contributions(cells, weight):
    shape = jax.ShapeDtypeStruct
    return pl.pallas_call(
        contribution_kernel,
        out_shape=(
            shape((6, 2, 32, LANES), F32),
            shape((6, 2, 32, LANES), F32),
            shape((128, 128), F32),
        ),
        in_specs=in_vmem(2),
        out_specs=tuple(in_vmem(3)),
        scratch_shapes=[pltpu.VMEM((3, 6, 32, 512), F32), pltpu.VMEM((128, 1024), BF16)],
        compiler_params=params(),
        cost_estimate=pl.CostEstimate(
            flops=300_000_000, bytes_accessed=2_000_000, transcendentals=0
        ),
        name="contributions",
    )(cells, weight)


def sums(core, left, own, right, back, corner, cells, square, weight):
    shape = jax.ShapeDtypeStruct
    return pl.pallas_call(
        sums_kernel,
        out_shape=(shape((2 * ROWS, LANES), F32), shape((2 * ROWS, LANES), F32)),
        in_specs=[pl.BlockSpec(memory_space=pltpu.SMEM)] + in_vmem(8),
        out_specs=tuple(in_vmem(2)),
        scratch_shapes=[
            pltpu.VMEM((96, 6144), BF16),
            pltpu.VMEM((96, 3072), BF16),
            pltpu.VMEM((6, 32, 512), F32),
            pltpu.VMEM((864, 1024), BF16),
            pltpu.VMEM((864, 1024), BF16),
            pltpu.VMEM((128, 1024), BF16),
            pltpu.VMEM((224, 1024), BF16),
            pltpu.VMEM((128, 1280), F32),
            pltpu.VMEM((224, 1280), F32),
        ],
        compiler_params=params(),
        cost_estimate=pl.CostEstimate(
            flops=3_000_000_000, bytes_accessed=6_000_000, transcendentals=200_000
        ),
        name="sums",
    )(core, left, own, right, back, corner, cells, square, weight)


def updates(total_cells, sums, order):
    return pl.pallas_call(
        functools.partial(root_kernel, total_cells),
        out_shape=jax.ShapeDtypeStruct((128, 864), F32),
        in_specs=in_vmem(2),
        out_specs=in_vmem(1)[0],
        scratch_shapes=[
            pltpu.VMEM((3, 96, 512), F32),
            pltpu.VMEM((864, 864), F32),
            pltpu.VMEM((864, 864), BF16),
        ],
        compiler_params=params(),
        cost_estimate=pl.CostEstimate(
            flops=8_000_000_000, bytes_accessed=6_000_000, transcendentals=1000
        ),
        name="updates",
    )(sums, order)


def on_device(density, weight_one, weight_two, cotangent):
    grid_x = lax.axis_size("y") * lax.axis_size("zh")
    grid_y = lax.axis_size("gc") * lax.axis_size("core")
    total_cells = 1024 * grid_x * grid_y
    core = lax.axis_index("core").astype(jnp.int32).reshape(1)

    def from_x(block, distance):
        pairs = [((i + distance) % grid_x, i) for i in range(grid_x)]
        return lax.ppermute(block, ("y", "zh"), pairs)

    def from_y(block, distance):
        pairs = [((i + distance) % grid_y, i) for i in range(grid_y)]
        return lax.ppermute(block, ("gc", "core"), pairs)

    def other_core(block):
        return lax.ppermute(block, "core", [(0, 1), (1, 0)])

    field = density.transpose(1, 2, 0, 3)
    field = jnp.concatenate([from_x(field[2:4], -1), field, from_x(field[0:2], 1)], axis=0)
    left = from_y(field, -1)
    right = from_y(field, 1)
    cells = cotangent.transpose(1, 2, 0, 3)
    kernel_one = weight_one.reshape(32, 32, 3, 3, 3).transpose(2, 3, 0, 4, 1).reshape(288, 96)
    kernel_two = weight_two.reshape(128, 32, 3, 3, 3).transpose(4, 2, 3, 1, 0).reshape(864, 128)
    back, beyond, square = contributions(cells, kernel_two)
    back = back + from_y(beyond, -1)
    corner = from_x(back[4:6], -1)
    keep, send = sums(core, left, field, right, back[0:4], corner, cells, square, kernel_one)
    both = keep + other_core(send)
    corr, grad = both[0:ROWS], both[ROWS : 2 * ROWS]
    group = lax.axis_size("y") * lax.axis_size("gc")
    chunk = ROWS // group

    def packed(corr, grad):
        high = lax.reduce_precision(grad, 8, 7)
        pieces = (corr.astype(BF16), high.astype(BF16), (grad - high).astype(BF16))
        return jnp.concatenate(
            [piece.reshape(-1, chunk, LANES) for piece in pieces], axis=1
        )

    def exchanged(parts, axes):
        return lax.all_to_all(parts, axes, 0, 0, tiled=True)

    def summed(parts):
        total = jnp.sum(parts.astype(F32), axis=0)
        return packed(total[0:chunk], total[chunk : 2 * chunk] + total[2 * chunk : 3 * chunk])

    def copies(part, count):
        return jnp.broadcast_to(part, (count, 3 * chunk, LANES))

    own = summed(exchanged(packed(corr, grad), ("y", "gc")))
    own = summed(exchanged(copies(own, lax.axis_size("zh")), "zh"))
    gathered = exchanged(copies(own, group), ("y", "gc"))
    mine = updates(float(total_cells), gathered, plane_order())
    other = other_core(mine)
    is_first = core[0] == 0
    update_one = jnp.where(is_first, mine[0:32], other[0:32])
    update_two = jnp.where(is_first, other, mine)
    return (update_one, update_two)


def solution(mesh):
    grid_x, grid_y = mesh.shape["gx"], mesh.shape["gy"]
    deep = max(grid_x // 4, 2)
    inner = Mesh(
        mesh.devices.reshape(grid_x // deep, deep, grid_y // 2, 2), ("y", "zh", "gc", "core")
    )
    split = P(None, ("y", "zh"), ("gc", "core"), None)
    return jax.shard_map(
        on_device,
        mesh=inner,
        in_specs=(split, P(), P(), split),
        out_specs=(P(), P()),
        check_vma=False,
    )
```

```python
import functools
import math

import jax
import jax.numpy as jnp
import numpy as np
from jax import lax
from jax.experimental import pallas as pl
from jax.experimental.pallas import tpu as pltpu
from jax.sharding import Mesh, PartitionSpec as P

ITERS = 3
DAMPING = 0.1
F32 = jnp.float32
BF16 = jnp.bfloat16
VMEM_LIMIT = 20 * 1024 * 1024
ROWS = 1024
LANES = 128


def dot_nt(left, right):
    return lax.dot_general(left, right, (((1,), (1,)), ((), ())), preferred_element_type=F32)


def dot_nn(left, right):
    return jnp.dot(left, right, preferred_element_type=F32)


def lane_ids(shape):
    return lax.broadcasted_iota(jnp.int32, shape, 1)


def from_below(values):
    return jnp.where(lane_ids(values.shape) == 0, 0.0, pltpu.roll(values, 1, 1))


def from_above(values):
    return jnp.where(
        lane_ids(values.shape) == LANES - 1, 0.0, pltpu.roll(values, LANES - 1, 1)
    )


def contribution_kernel(cells_ref, weight_ref, rest_ref, send_ref, square_ref, acc_ref, flat_ref):
    weight = weight_ref[...]
    acc_ref[...] = jnp.zeros_like(acc_ref)
    for x in range(4):
        for y in range(2):
            place = slice((x * 2 + y) * LANES, (x * 2 + y + 1) * LANES)
            flat_ref[:, place] = cells_ref[x, y]
        terms = dot_nn(weight, flat_ref[:, x * 256 : (x + 1) * 256])
        for e in range(3):
            for a in range(3):
                for b in range(3):
                    first = (9 * e + 3 * a + b) * 32
                    lanes = slice(b * LANES, (b + 2) * LANES)
                    acc_ref[e, x + a, :, lanes] = (
                        acc_ref[e, x + a, :, lanes] + terms[first : first + 32]
                    )
    for row in range(6):
        for y in range(4):
            lanes = slice(y * LANES, (y + 1) * LANES)
            total = (
                from_above(acc_ref[0, row, :, lanes])
                + acc_ref[1, row, :, lanes]
                + from_below(acc_ref[2, row, :, lanes])
            )
            if y < 2:
                rest_ref[row, y] = total
            else:
                send_ref[row, y - 2] = total
    cells = flat_ref[...]
    square_ref[...] = dot_nt(cells, cells)


def stacked_products(signal_ref, stack_ref, corr_ref, grad_ref):
    corr_ref[:, 0:864] = dot_nt(stack_ref[0:96, :], stack_ref[...])
    lower = stack_ref[96:288, :]
    first = dot_nt(lower, stack_ref[288:384, :])
    second = dot_nt(lower, stack_ref[576:672, :])
    corr_ref[:, 864:960] = first[0:96]
    corr_ref[:, 960:1056] = first[96:192]
    corr_ref[:, 1056:1152] = second[0:96]
    corr_ref[:, 1152:1248] = second[96:192]
    corr_ref[:, 1248:1280] = jnp.zeros((96, 32), F32)
    grad_ref[...] = dot_nt(stack_ref[...], signal_ref[...])


def sums_kernel(
    core_ref, left_ref, own_ref, right_ref, back_ref, corner_ref, cells_ref, square_ref, weight_ref,
    keep_ref, send_ref,
    shifted_ref, hidden_ref, acc_ref, stack_one_ref, stack_two_ref,
    signal_ref, flat_ref, corr_one_ref, corr_two_ref, grad_one_ref, grad_two_ref,
):
    parts = (left_ref, own_ref, right_ref)
    for x in range(8):
        for y in range(6):
            column = parts[y // 2][x, y % 2].astype(F32)
            lanes = slice((x * 6 + y) * LANES, (x * 6 + y + 1) * LANES)
            shifted_ref[0:32, lanes] = from_below(column).astype(BF16)
            shifted_ref[32:64, lanes] = column.astype(BF16)
            shifted_ref[64:96, lanes] = from_above(column).astype(BF16)
    weight = weight_ref[...]
    acc_ref[...] = jnp.zeros_like(acc_ref)
    for x in range(8):
        terms = dot_nn(weight, shifted_ref[:, x * 768 : (x + 1) * 768])
        for a in range(3):
            row = x - a + 1
            if 1 <= row <= 6:
                total = acc_ref[row - 1]
                for b in range(3):
                    first = (3 * a + b) * 32
                    total = total + terms[first : first + 32, b * LANES : b * LANES + 512]
                acc_ref[row - 1] = total
    signal_ref[32:128, :] = jnp.zeros((96, 1024), BF16)
    for row in range(6):
        linear = acc_ref[row]
        logistic = 1.0 / (1.0 + jnp.exp(-linear))
        hidden = (linear * logistic).astype(BF16).astype(F32)
        for y in range(4):
            column = hidden[:, y * LANES : (y + 1) * LANES]
            lanes = slice((row * 4 + y) * LANES, (row * 4 + y + 1) * LANES)
            hidden_ref[0:32, lanes] = from_below(column).astype(BF16)
            hidden_ref[32:64, lanes] = column.astype(BF16)
            hidden_ref[64:96, lanes] = from_above(column).astype(BF16)
        if row < 4:
            slope = logistic * (1.0 + linear * (1.0 - logistic))
            for y in range(2):
                back = back_ref[row, y]
                if row < 2:
                    back = back + corner_ref[row, y]
                place = slice((row * 2 + y) * LANES, (row * 2 + y + 1) * LANES)
                signal = back * slope[:, y * LANES : (y + 1) * LANES]
                signal_ref[0:32, place] = signal.astype(BF16)
                flat_ref[:, place] = cells_ref[row, y]
    for a in range(3):
        for b in range(3):
            rows = slice((3 * a + b) * 96, (3 * a + b + 1) * 96)
            for x in range(4):
                lanes = slice(x * 256, (x + 1) * 256)
                one = ((x + a) * 6 + b) * LANES
                two = ((x + a) * 4 + b) * LANES
                stack_one_ref[rows, lanes] = shifted_ref[:, one : one + 256]
                stack_two_ref[rows, lanes] = hidden_ref[:, two : two + 256]
    stacked_products(signal_ref, stack_one_ref, corr_one_ref, grad_one_ref)
    stacked_products(flat_ref, stack_two_ref, corr_two_ref, grad_two_ref)
    signal = signal_ref[...]
    square_one = dot_nt(signal, signal)
    is_first = core_ref[0] == 0

    def put(first, one, two):
        rows = slice(first, first + one.shape[0])
        keep_ref[rows, :] = jnp.where(is_first, one, two)
        send_ref[rows, :] = jnp.where(is_first, two, one)

    for tile in range(10):
        lanes = slice(tile * LANES, (tile + 1) * LANES)
        put(tile * 96, corr_one_ref[:, lanes], corr_two_ref[:, lanes])
    put(ROWS, grad_one_ref[...], grad_two_ref[...])
    put(ROWS + 864, square_one, square_ref[...])
    for first, last in ((960, ROWS), (ROWS + 992, 2 * ROWS)):
        keep_ref[first:last, :] = jnp.zeros((last - first, LANES), F32)
        send_ref[first:last, :] = jnp.zeros((last - first, LANES), F32)


def split_product(left, right):
    high = right.astype(BF16)
    low = (right - high.astype(F32)).astype(BF16)
    product = dot_nn(left, jnp.concatenate([high, low], axis=1))
    return product[:, 0:LANES] + product[:, LANES : 2 * LANES]


def root_kernel(total_cells, sums_ref, order_ref, out_ref, strip_ref, full_ref, factor_ref):
    count, triple, _ = sums_ref.shape
    values = sums_ref[...].astype(F32).reshape(count, 3, triple // 3, LANES)
    corr = values[:, 0].reshape(ROWS, LANES)
    grads = (values[:, 1] + values[:, 2]).reshape(ROWS, LANES)
    corr = jnp.concatenate([corr[96 * j : 96 * j + 96] for j in range(10)], axis=1)
    gradient = grads[0:864]

    def identity(order, dtype):
        rows = lax.broadcasted_iota(jnp.int32, (order, order), 0)
        return jnp.where(rows == lane_ids((order, order)), 1.0, 0.0).astype(dtype)

    eye_96 = identity(96, BF16)
    eye_288 = identity(288, BF16)
    strip_ref[0, :, 0:96] = dot_nt(eye_96, corr[:, 192:288].astype(BF16))
    strip_ref[0, :, 96:192] = dot_nt(eye_96, corr[:, 96:192].astype(BF16))
    strip_ref[0, :, 192:480] = corr[:, 0:288]
    strip_ref[1, :, 0:96] = corr[:, 960:1056]
    strip_ref[1, :, 96:192] = corr[:, 864:960]
    strip_ref[1, :, 192:480] = corr[:, 288:576]
    strip_ref[2, :, 0:96] = corr[:, 1152:1248]
    strip_ref[2, :, 96:192] = corr[:, 1056:1152]
    strip_ref[2, :, 192:480] = corr[:, 576:864]
    for b in range(3):
        for step in range(3):
            piece = strip_ref[step, :, (2 - b) * 96 : (2 - b) * 96 + 288]
            for a in range(3 - step):
                first = a * 288 + b * 96
                full_ref[first : first + 96, (a + step) * 288 : (a + step + 1) * 288] = piece
    turned_one = dot_nt(eye_288, full_ref[0:288, 288:576].astype(BF16))
    turned_two = dot_nt(eye_288, full_ref[0:288, 576:864].astype(BF16))
    full_ref[288:576, 0:288] = turned_one
    full_ref[576:864, 288:576] = turned_one
    full_ref[576:864, 0:288] = turned_two
    whole = full_ref[...]
    factor_ref[...] = whole.astype(BF16)
    bound = jnp.max(jnp.sum(jnp.abs(whole), axis=0, keepdims=True)) / total_cells + DAMPING
    scale = 1.0 / (bound * total_cells)
    shift = DAMPING / bound

    def times(columns):
        return split_product(factor_ref[...], columns) * scale + columns * shift

    def once(columns):
        return 1.5 * columns - 0.5 * times(columns)

    def iterate(columns, step):
        if step == 0:
            return once(columns)
        first = iterate(columns, step - 1)
        second = iterate(iterate(times(first), step - 1), step - 1)
        return 1.5 * first - 0.5 * second

    right = iterate(gradient, ITERS - 1)

    eye_128 = identity(128, F32)
    small = grads[864:992] / total_cells + DAMPING * eye_128
    small_bound = jnp.max(jnp.sum(jnp.abs(small), axis=0, keepdims=True))
    scaled = small / small_bound
    root = 1.5 * eye_128 - 0.5 * scaled
    exact = functools.partial(
        jnp.dot, precision=lax.Precision.HIGHEST, preferred_element_type=F32
    )
    for _ in range(ITERS - 1):
        product = exact(exact(exact(root, scaled), root), root)
        root = 1.5 * root - 0.5 * product
    factor = 1.0 / (math.sqrt(total_cells) * jnp.sqrt(small_bound) * jnp.sqrt(bound))
    update = exact(right, root) * factor
    out_ref[...] = split_product(order_ref[...], update)


def plane_order():
    order = np.zeros((864, 864), np.float32)
    for offset in range(27):
        for channel in range(32):
            order[channel * 27 + offset, offset * 32 + channel] = 1.0
    return jnp.asarray(order, BF16)


def params():
    return pltpu.CompilerParams(vmem_limit_bytes=VMEM_LIMIT)


def in_vmem(count):
    return [pl.BlockSpec(memory_space=pltpu.VMEM)] * count


def contributions(cells, weight):
    shape = jax.ShapeDtypeStruct
    return pl.pallas_call(
        contribution_kernel,
        out_shape=(
            shape((6, 2, 32, LANES), F32),
            shape((6, 2, 32, LANES), F32),
            shape((128, 128), F32),
        ),
        in_specs=in_vmem(2),
        out_specs=tuple(in_vmem(3)),
        scratch_shapes=[pltpu.VMEM((3, 6, 32, 512), F32), pltpu.VMEM((128, 1024), BF16)],
        compiler_params=params(),
        cost_estimate=pl.CostEstimate(
            flops=300_000_000, bytes_accessed=2_000_000, transcendentals=0
        ),
        name="contributions",
    )(cells, weight)


def sums(core, left, own, right, back, corner, cells, square, weight):
    shape = jax.ShapeDtypeStruct
    return pl.pallas_call(
        sums_kernel,
        out_shape=(shape((2 * ROWS, LANES), F32), shape((2 * ROWS, LANES), F32)),
        in_specs=[pl.BlockSpec(memory_space=pltpu.SMEM)] + in_vmem(8),
        out_specs=tuple(in_vmem(2)),
        scratch_shapes=[
            pltpu.VMEM((96, 6144), BF16),
            pltpu.VMEM((96, 3072), BF16),
            pltpu.VMEM((6, 32, 512), F32),
            pltpu.VMEM((864, 1024), BF16),
            pltpu.VMEM((864, 1024), BF16),
            pltpu.VMEM((128, 1024), BF16),
            pltpu.VMEM((128, 1024), BF16),
            pltpu.VMEM((96, 1280), F32),
            pltpu.VMEM((96, 1280), F32),
            pltpu.VMEM((864, 128), F32),
            pltpu.VMEM((864, 128), F32),
        ],
        compiler_params=params(),
        cost_estimate=pl.CostEstimate(
            flops=3_000_000_000, bytes_accessed=6_000_000, transcendentals=200_000
        ),
        name="sums",
    )(core, left, own, right, back, corner, cells, square, weight)


def updates(total_cells, sums, order):
    return pl.pallas_call(
        functools.partial(root_kernel, total_cells),
        out_shape=jax.ShapeDtypeStruct((864, 128), F32),
        in_specs=in_vmem(2),
        out_specs=in_vmem(1)[0],
        scratch_shapes=[
            pltpu.VMEM((3, 96, 512), F32),
            pltpu.VMEM((864, 864), F32),
            pltpu.VMEM((864, 864), BF16),
        ],
        compiler_params=params(),
        cost_estimate=pl.CostEstimate(
            flops=8_000_000_000, bytes_accessed=6_000_000, transcendentals=1000
        ),
        name="updates",
    )(sums, order)


def on_device(density, weight_one, weight_two, cotangent):
    grid_x = lax.axis_size("y") * lax.axis_size("zh")
    grid_y = lax.axis_size("gc") * lax.axis_size("core")
    total_cells = 1024 * grid_x * grid_y
    core = lax.axis_index("core").astype(jnp.int32).reshape(1)

    def from_x(block, distance):
        pairs = [((i + distance) % grid_x, i) for i in range(grid_x)]
        return lax.ppermute(block, ("y", "zh"), pairs)

    def from_y(block, distance):
        pairs = [((i + distance) % grid_y, i) for i in range(grid_y)]
        return lax.ppermute(block, ("gc", "core"), pairs)

    def other_core(block):
        return lax.ppermute(block, "core", [(0, 1), (1, 0)])

    field = density.transpose(1, 2, 0, 3)
    after = from_x(field[0:2], 1)
    cells = cotangent.transpose(1, 2, 0, 3)
    kernel_one = weight_one.reshape(32, 32, 3, 3, 3).transpose(2, 3, 0, 4, 1).reshape(288, 96)
    kernel_two = weight_two.reshape(128, 32, 3, 3, 3).transpose(4, 2, 3, 1, 0).reshape(864, 128)
    back, beyond, square = contributions(cells, kernel_two)
    last_rows, beyond = lax.optimization_barrier((field[2:4], beyond))
    beyond = from_y(beyond, -1)
    field = jnp.concatenate([from_x(last_rows, -1), field, after], axis=0)
    left = from_y(field, -1)
    right = from_y(field, 1)
    back = back + beyond
    corner = from_x(back[4:6], -1)
    keep, send = sums(core, left, field, right, back[0:4], corner, cells, square, kernel_one)
    both = keep + other_core(send)
    corr, grad = both[0:ROWS], both[ROWS : 2 * ROWS]
    group = lax.axis_size("y") * lax.axis_size("gc")
    chunk = ROWS // group

    def packed(corr, grad):
        high = lax.reduce_precision(grad, 8, 7)
        pieces = (corr.astype(BF16), high.astype(BF16), (grad - high).astype(BF16))
        return jnp.concatenate(
            [piece.reshape(-1, chunk, LANES) for piece in pieces], axis=1
        )

    def exchanged(parts, axes):
        return lax.all_to_all(parts, axes, 0, 0, tiled=True)

    def summed(parts):
        total = jnp.sum(parts.astype(F32), axis=0)
        return packed(total[0:chunk], total[chunk : 2 * chunk] + total[2 * chunk : 3 * chunk])

    def copies(part, count):
        return jnp.broadcast_to(part, (count, 3 * chunk, LANES))

    own = summed(exchanged(packed(corr, grad), ("y", "gc")))
    own = summed(exchanged(copies(own, lax.axis_size("zh")), "zh"))
    gathered = exchanged(copies(own, group), ("y", "gc"))
    mine = updates(float(total_cells), gathered, plane_order())
    other = other_core(mine)
    is_first = core[0] == 0
    update_one = jnp.where(is_first, mine[:, 0:32], other[:, 0:32]).T
    update_two = jnp.where(is_first, other, mine).T
    return (update_one, update_two)


def solution(mesh):
    grid_x, grid_y = mesh.shape["gx"], mesh.shape["gy"]
    deep = max(grid_x // 4, 2)
    inner = Mesh(
        mesh.devices.reshape(grid_x // deep, deep, grid_y // 2, 2), ("y", "zh", "gc", "core")
    )
    split = P(None, ("y", "zh"), ("gc", "core"), None)
    return jax.shard_map(
        on_device,
        mesh=inner,
        in_specs=(split, P(), P(), split),
        out_specs=(P(), P()),
        check_vma=False,
    )
```

```python
import functools
import math

import jax
import jax.numpy as jnp
import numpy as np
from jax import lax
from jax.experimental import pallas as pl
from jax.experimental.pallas import tpu as pltpu
from jax.sharding import Mesh, PartitionSpec as P

ITERS = 3
DAMPING = 0.1
F32 = jnp.float32
BF16 = jnp.bfloat16
VMEM_LIMIT = 20 * 1024 * 1024
ROWS = 1024
LANES = 128


def dot_nt(left, right):
    return lax.dot_general(left, right, (((1,), (1,)), ((), ())), preferred_element_type=F32)


def dot_nn(left, right):
    return jnp.dot(left, right, preferred_element_type=F32)


def lane_ids(shape):
    return lax.broadcasted_iota(jnp.int32, shape, 1)


def from_below(values):
    return jnp.where(lane_ids(values.shape) == 0, 0.0, pltpu.roll(values, 1, 1))


def from_above(values):
    return jnp.where(
        lane_ids(values.shape) == LANES - 1, 0.0, pltpu.roll(values, LANES - 1, 1)
    )


def contribution_kernel(cells_ref, weight_ref, rest_ref, send_ref, square_ref, acc_ref, flat_ref):
    weight = weight_ref[...]
    acc_ref[...] = jnp.zeros_like(acc_ref)
    for x in range(4):
        for y in range(2):
            place = slice((x * 2 + y) * LANES, (x * 2 + y + 1) * LANES)
            flat_ref[:, place] = cells_ref[x, y]
        terms = dot_nn(weight, flat_ref[:, x * 256 : (x + 1) * 256])
        for e in range(3):
            for a in range(3):
                for b in range(3):
                    first = (9 * e + 3 * a + b) * 32
                    lanes = slice(b * LANES, (b + 2) * LANES)
                    acc_ref[e, x + a, :, lanes] = (
                        acc_ref[e, x + a, :, lanes] + terms[first : first + 32]
                    )
    for row in range(6):
        for y in range(4):
            lanes = slice(y * LANES, (y + 1) * LANES)
            total = (
                from_above(acc_ref[0, row, :, lanes])
                + acc_ref[1, row, :, lanes]
                + from_below(acc_ref[2, row, :, lanes])
            )
            if y < 2:
                rest_ref[row, y] = total
            else:
                send_ref[row, y - 2] = total
    cells = flat_ref[...]
    square_ref[...] = dot_nt(cells, cells)


def stacked_products(left_ref, stack_ref, out_ref):
    out_ref[:, 0:864] = dot_nt(left_ref[...], stack_ref[...])
    lower = stack_ref[96:288, :]
    first = dot_nt(lower, stack_ref[288:384, :])
    second = dot_nt(lower, stack_ref[576:672, :])
    out_ref[0:96, 864:960] = first[0:96]
    out_ref[0:96, 960:1056] = first[96:192]
    out_ref[0:96, 1056:1152] = second[0:96]
    out_ref[0:96, 1152:1248] = second[96:192]
    out_ref[0:96, 1248:1280] = jnp.zeros((96, 32), F32)


def sums_kernel(
    core_ref, inner_ref, own_ref, outer_ref, back_ref, corner_ref, cells_ref, square_ref, weight_ref,
    keep_ref, send_ref,
    shifted_ref, hidden_ref, acc_ref, stack_one_ref, stack_two_ref,
    rows_one_ref, rows_two_ref, out_one_ref, out_two_ref,
):
    is_first = core_ref[0] == 0
    for x in range(8):
        for y in range(6):
            if 2 <= y < 4:
                column = own_ref[x, y - 2].astype(F32)
            else:
                inner = inner_ref[x, y % 2].astype(F32)
                outer = outer_ref[x, y % 2].astype(F32)
                column = jnp.where(is_first == (y < 2), outer, inner)
            lanes = slice((x * 6 + y) * LANES, (x * 6 + y + 1) * LANES)
            shifted_ref[0:32, lanes] = from_below(column).astype(BF16)
            shifted_ref[32:64, lanes] = column.astype(BF16)
            shifted_ref[64:96, lanes] = from_above(column).astype(BF16)
    weight = weight_ref[...]
    acc_ref[...] = jnp.zeros_like(acc_ref)
    for x in range(8):
        terms = dot_nn(weight, shifted_ref[:, x * 768 : (x + 1) * 768])
        for a in range(3):
            row = x - a + 1
            if 1 <= row <= 6:
                total = acc_ref[row - 1]
                for b in range(3):
                    first = (3 * a + b) * 32
                    total = total + terms[first : first + 32, b * LANES : b * LANES + 512]
                acc_ref[row - 1] = total
    for row in range(6):
        linear = acc_ref[row]
        logistic = 1.0 / (1.0 + jnp.exp(-linear))
        hidden = (linear * logistic).astype(BF16).astype(F32)
        for y in range(4):
            column = hidden[:, y * LANES : (y + 1) * LANES]
            lanes = slice((row * 4 + y) * LANES, (row * 4 + y + 1) * LANES)
            hidden_ref[0:32, lanes] = from_below(column).astype(BF16)
            hidden_ref[32:64, lanes] = column.astype(BF16)
            hidden_ref[64:96, lanes] = from_above(column).astype(BF16)
        if row < 4:
            slope = logistic * (1.0 + linear * (1.0 - logistic))
            for y in range(2):
                back = back_ref[row, y]
                if row < 2:
                    back = back + corner_ref[row, y]
                place = slice((row * 2 + y) * LANES, (row * 2 + y + 1) * LANES)
                signal = back * slope[:, y * LANES : (y + 1) * LANES]
                rows_one_ref[96:128, place] = signal.astype(BF16)
                rows_two_ref[96:224, place] = cells_ref[row, y]
    for a in range(3):
        for b in range(3):
            rows = slice((3 * a + b) * 96, (3 * a + b + 1) * 96)
            for x in range(4):
                lanes = slice(x * 256, (x + 1) * 256)
                one = ((x + a) * 6 + b) * LANES
                two = ((x + a) * 4 + b) * LANES
                stack_one_ref[rows, lanes] = shifted_ref[:, one : one + 256]
                stack_two_ref[rows, lanes] = hidden_ref[:, two : two + 256]
    rows_one_ref[0:96, :] = stack_one_ref[0:96, :]
    rows_two_ref[0:96, :] = stack_two_ref[0:96, :]
    stacked_products(rows_one_ref, stack_one_ref, out_one_ref)
    stacked_products(rows_two_ref, stack_two_ref, out_two_ref)
    signal = rows_one_ref[96:128, :]
    square_one = dot_nt(signal, signal)

    def put(rows, one, two):
        keep_ref[rows, :] = jnp.where(is_first, one, two)
        send_ref[rows, :] = jnp.where(is_first, two, one)

    for tile in range(10):
        lanes = slice(tile * LANES, (tile + 1) * LANES)
        put(
            slice(tile * 96, (tile + 1) * 96), out_one_ref[0:96, lanes], out_two_ref[0:96, lanes]
        )
    nothing = jnp.zeros((96, LANES), F32)
    keep_ref[960:ROWS, :] = nothing[0 : ROWS - 960]
    send_ref[960:ROWS, :] = nothing[0 : ROWS - 960]
    for tile in range(7):
        lanes = slice(tile * LANES, (tile + 1) * LANES)
        one = out_one_ref[96:128, lanes]
        two = out_two_ref[96:224, lanes]
        if tile == 6:
            one = jnp.where(lane_ids(one.shape) < 96, one, 0.0)
            two = jnp.where(lane_ids(two.shape) < 96, two, 0.0)
        put(
            slice(ROWS + tile * 128, ROWS + (tile + 1) * 128),
            jnp.concatenate([one, nothing], axis=0),
            two,
        )
    wide = jnp.concatenate([square_one, jnp.zeros((32, 96), F32)], axis=1)
    put(
        slice(ROWS + 896, ROWS + 1024), jnp.concatenate([wide, nothing], axis=0), square_ref[...]
    )


def split_rows(values):
    high = values.astype(BF16)
    low = (values - high.astype(F32)).astype(BF16)
    return jnp.concatenate([high, low], axis=0)


def root_kernel(total_cells, core_ref, sums_ref, order_ref, out_ref, strip_ref, full_ref, factor_ref):
    count, triple, _ = sums_ref.shape
    values = sums_ref[...].astype(F32).reshape(count, 3, triple // 3, LANES)
    corr = values[:, 0].reshape(ROWS, LANES)
    grads = (values[:, 1] + values[:, 2]).reshape(ROWS, LANES)
    corr = jnp.concatenate([corr[96 * j : 96 * j + 96] for j in range(10)], axis=1)
    gradient = jnp.concatenate([grads[128 * j : 128 * j + 128] for j in range(7)], axis=1)[:, 0:864]

    def identity(order, dtype):
        rows = lax.broadcasted_iota(jnp.int32, (order, order), 0)
        return jnp.where(rows == lane_ids((order, order)), 1.0, 0.0).astype(dtype)

    eye_96 = identity(96, BF16)
    eye_288 = identity(288, BF16)
    strip_ref[0, :, 0:96] = dot_nt(eye_96, corr[:, 192:288].astype(BF16))
    strip_ref[0, :, 96:192] = dot_nt(eye_96, corr[:, 96:192].astype(BF16))
    strip_ref[0, :, 192:480] = corr[:, 0:288]
    strip_ref[1, :, 0:96] = corr[:, 960:1056]
    strip_ref[1, :, 96:192] = corr[:, 864:960]
    strip_ref[1, :, 192:480] = corr[:, 288:576]
    strip_ref[2, :, 0:96] = corr[:, 1152:1248]
    strip_ref[2, :, 96:192] = corr[:, 1056:1152]
    strip_ref[2, :, 192:480] = corr[:, 576:864]
    for b in range(3):
        for step in range(3):
            piece = strip_ref[step, :, (2 - b) * 96 : (2 - b) * 96 + 288]
            for a in range(3 - step):
                first = a * 288 + b * 96
                full_ref[first : first + 96, (a + step) * 288 : (a + step + 1) * 288] = piece
    turned_one = dot_nt(eye_288, full_ref[0:288, 288:576].astype(BF16))
    turned_two = dot_nt(eye_288, full_ref[0:288, 576:864].astype(BF16))
    full_ref[288:576, 0:288] = turned_one
    full_ref[576:864, 288:576] = turned_one
    full_ref[576:864, 0:288] = turned_two
    whole = full_ref[...]
    factor_ref[...] = whole.astype(BF16)
    bound = jnp.max(jnp.sum(jnp.abs(whole), axis=0, keepdims=True)) / total_cells + DAMPING
    scale = 1.0 / (bound * total_cells)
    shift = DAMPING / bound

    def times(rows):
        product = dot_nn(split_rows(rows), factor_ref[...])
        return (product[0:128] + product[128:256]) * scale + rows * shift

    def once(rows):
        return 1.5 * rows - 0.5 * times(rows)

    def iterate(rows, step):
        if step == 0:
            return once(rows)
        first = iterate(rows, step - 1)
        second = iterate(iterate(times(first), step - 1), step - 1)
        return 1.5 * first - 0.5 * second

    right = iterate(gradient, ITERS - 1)

    eye_128 = identity(128, F32)
    small = grads[896:1024] / total_cells + DAMPING * eye_128
    small_bound = jnp.max(jnp.sum(jnp.abs(small), axis=0, keepdims=True))
    scaled = small / small_bound
    root = 1.5 * eye_128 - 0.5 * scaled
    for _ in range(ITERS - 1):
        product = square_product(square_product(square_product(root, scaled), root), root)
        root = 1.5 * root - 0.5 * product
    factor = 1.0 / (math.sqrt(total_cells) * jnp.sqrt(small_bound) * jnp.sqrt(bound))
    both = split_rows(root)
    high = right.astype(BF16)
    low = (right - high.astype(F32)).astype(BF16)
    update = dot_nn(both, high)
    update = (update[0:128] + update[128:256] + dot_nn(both[0:128], low)) * factor
    ordered = dot_nn(split_rows(update), order_ref[...])
    ordered = ordered[0:128] + ordered[128:256]
    ordered = jnp.concatenate([ordered, jnp.zeros((128, 32), F32)], axis=1)
    is_first = core_ref[0] == 0
    for tile in range(7):
        piece = ordered[:, tile * LANES : (tile + 1) * LANES]
        turned = piece.T
        out_ref[tile * 128 : min(tile * 128 + 128, 864), :] = turned[0 : min(128, 864 - tile * 128)]

    @pl.when(is_first)
    def _():
        for tile in range(7):
            out_ref[tile * 32 : tile * 32 + 32, :] = ordered[
                0:32, tile * LANES : (tile + 1) * LANES
            ]


def square_product(left, right):
    high = right.astype(BF16)
    low = (right - high.astype(F32)).astype(BF16)
    product = dot_nn(split_rows(left), jnp.concatenate([high, low], axis=1))
    return product[0:128, 0:128] + product[0:128, 128:256] + product[128:256, 0:128]


def pick_kernel(core_ref, mine_ref, other_ref, one_ref, two_ref):
    is_first = core_ref[0] == 0
    for tile in range(7):
        rows = slice(tile * 32, tile * 32 + 32)
        piece = jnp.where(is_first, mine_ref[rows, :], other_ref[rows, :])
        width = min(LANES, 864 - tile * LANES)
        one_ref[:, tile * LANES : tile * LANES + width] = piece[:, 0:width]
    two_ref[...] = jnp.where(is_first, other_ref[...], mine_ref[...])


def plane_order():
    order = np.zeros((864, 864), np.float32)
    for offset in range(27):
        for channel in range(32):
            order[offset * 32 + channel, channel * 27 + offset] = 1.0
    return jnp.asarray(order, BF16)


def params():
    return pltpu.CompilerParams(vmem_limit_bytes=VMEM_LIMIT)


def in_vmem(count):
    return [pl.BlockSpec(memory_space=pltpu.VMEM)] * count


def contributions(cells, weight):
    shape = jax.ShapeDtypeStruct
    return pl.pallas_call(
        contribution_kernel,
        out_shape=(
            shape((6, 2, 32, LANES), F32),
            shape((6, 2, 32, LANES), F32),
            shape((128, 128), F32),
        ),
        in_specs=in_vmem(2),
        out_specs=tuple(in_vmem(3)),
        scratch_shapes=[pltpu.VMEM((3, 6, 32, 512), F32), pltpu.VMEM((128, 1024), BF16)],
        compiler_params=params(),
        cost_estimate=pl.CostEstimate(
            flops=300_000_000, bytes_accessed=2_000_000, transcendentals=0
        ),
        name="contributions",
    )(cells, weight)


def sums(core, left, own, right, back, corner, cells, square, weight):
    shape = jax.ShapeDtypeStruct
    return pl.pallas_call(
        sums_kernel,
        out_shape=(shape((2 * ROWS, LANES), F32), shape((2 * ROWS, LANES), F32)),
        in_specs=[pl.BlockSpec(memory_space=pltpu.SMEM)] + in_vmem(8),
        out_specs=tuple(in_vmem(2)),
        scratch_shapes=[
            pltpu.VMEM((96, 6144), BF16),
            pltpu.VMEM((96, 3072), BF16),
            pltpu.VMEM((6, 32, 512), F32),
            pltpu.VMEM((864, 1024), BF16),
            pltpu.VMEM((864, 1024), BF16),
            pltpu.VMEM((128, 1024), BF16),
            pltpu.VMEM((224, 1024), BF16),
            pltpu.VMEM((128, 1280), F32),
            pltpu.VMEM((224, 1280), F32),
        ],
        compiler_params=params(),
        cost_estimate=pl.CostEstimate(
            flops=3_000_000_000, bytes_accessed=6_000_000, transcendentals=200_000
        ),
        name="sums",
    )(core, left, own, right, back, corner, cells, square, weight)


def updates(total_cells, core, sums, order):
    return pl.pallas_call(
        functools.partial(root_kernel, total_cells),
        out_shape=jax.ShapeDtypeStruct((864, 128), F32),
        in_specs=[pl.BlockSpec(memory_space=pltpu.SMEM)] + in_vmem(2),
        out_specs=in_vmem(1)[0],
        scratch_shapes=[
            pltpu.VMEM((3, 96, 512), F32),
            pltpu.VMEM((864, 864), F32),
            pltpu.VMEM((864, 864), BF16),
        ],
        compiler_params=params(),
        cost_estimate=pl.CostEstimate(
            flops=8_000_000_000, bytes_accessed=6_000_000, transcendentals=1000
        ),
        name="updates",
    )(core, sums, order)


def picked(core, mine, other):
    shape = jax.ShapeDtypeStruct
    return pl.pallas_call(
        pick_kernel,
        out_shape=(shape((32, 864), F32), shape((864, 128), F32)),
        in_specs=[pl.BlockSpec(memory_space=pltpu.SMEM)] + in_vmem(2),
        compiler_params=params(),
        name="picked",
    )(core, mine, other)


def pairs(count, offset):
    return [(i, (i + 1 if (i - offset) % 2 == 0 else i - 1) % count) for i in range(count)]


def on_device(density, weight_one, weight_two, cotangent):
    grid_x = lax.axis_size("y") * lax.axis_size("zh")
    grid_y = lax.axis_size("gc") * lax.axis_size("core")
    total_cells = 1024 * grid_x * grid_y
    core = lax.axis_index("core").astype(jnp.int32).reshape(1)

    def from_x(block, distance):
        pairs = [((i + distance) % grid_x, i) for i in range(grid_x)]
        return lax.ppermute(block, ("y", "zh"), pairs)

    def from_y(block, distance):
        pairs = [((i + distance) % grid_y, i) for i in range(grid_y)]
        return lax.ppermute(block, ("gc", "core"), pairs)

    def other_core(block):
        return lax.ppermute(block, "core", [(0, 1), (1, 0)])

    field = density.transpose(1, 2, 0, 3)
    low, high = field[0:2], field[2:4]
    even = lax.axis_index("zh") % 2 == 0
    first = lax.ppermute(jnp.where(even, high, low), ("y", "zh"), pairs(grid_x, 0))
    second = lax.ppermute(jnp.where(even, low, high), ("y", "zh"), pairs(grid_x, 1))
    field = jnp.concatenate(
        [jnp.where(even, second, first), field, jnp.where(even, first, second)], axis=0
    )
    inner = other_core(field)
    outer = lax.ppermute(field, ("gc", "core"), pairs(grid_y, 1))
    cells = cotangent.transpose(1, 2, 0, 3)
    kernel_one = weight_one.reshape(32, 32, 3, 3, 3).transpose(2, 3, 0, 4, 1).reshape(288, 96)
    kernel_two = weight_two.reshape(128, 32, 3, 3, 3).transpose(4, 2, 3, 1, 0).reshape(864, 128)
    back, beyond, square = contributions(cells, kernel_two)
    back = back + from_y(beyond, -1)
    corner = from_x(back[4:6], -1)
    keep, send = sums(core, inner, field, outer, back[0:4], corner, cells, square, kernel_one)
    both = keep + other_core(send)
    corr, grad = both[0:ROWS], both[ROWS : 2 * ROWS]
    group = lax.axis_size("y") * lax.axis_size("gc")
    chunk = ROWS // group

    def packed(corr, grad):
        high = lax.reduce_precision(grad, 8, 7)
        pieces = (corr.astype(BF16), high.astype(BF16), (grad - high).astype(BF16))
        return jnp.concatenate(
            [piece.reshape(-1, chunk, LANES) for piece in pieces], axis=1
        )

    def exchanged(parts, axes):
        return lax.all_to_all(parts, axes, 0, 0, tiled=True)

    def summed(parts):
        total = jnp.sum(parts.astype(F32), axis=0)
        return packed(total[0:chunk], total[chunk : 2 * chunk] + total[2 * chunk : 3 * chunk])

    def copies(part, count):
        return jnp.broadcast_to(part, (count, 3 * chunk, LANES))

    own = summed(exchanged(packed(corr, grad), ("y", "gc")))
    own = summed(exchanged(copies(own, lax.axis_size("zh")), "zh"))
    gathered = exchanged(copies(own, group), ("y", "gc"))
    mine = updates(float(total_cells), core, gathered, plane_order())
    update_one, update_two = picked(core, mine, other_core(mine))
    return (update_one, update_two.T)


def solution(mesh):
    grid_x, grid_y = mesh.shape["gx"], mesh.shape["gy"]
    deep = max(grid_x // 4, 2)
    inner = Mesh(
        mesh.devices.reshape(grid_x // deep, deep, grid_y // 2, 2), ("y", "zh", "gc", "core")
    )
    split = P(None, ("y", "zh"), ("gc", "core"), None)
    return jax.shard_map(
        on_device,
        mesh=inner,
        in_specs=(split, P(), P(), split),
        out_specs=(P(), P()),
        check_vma=False,
    )
```

```python
import functools
import math

import jax
import jax.numpy as jnp
import numpy as np
from jax import lax
from jax.experimental import pallas as pl
from jax.experimental.pallas import tpu as pltpu
from jax.sharding import Mesh, PartitionSpec as P

ITERS = 3
DAMPING = 0.1
F32 = jnp.float32
BF16 = jnp.bfloat16
VMEM_LIMIT = 20 * 1024 * 1024
ROWS = 1024
LANES = 128


def dot_nt(left, right):
    return lax.dot_general(left, right, (((1,), (1,)), ((), ())), preferred_element_type=F32)


def dot_nn(left, right):
    return jnp.dot(left, right, preferred_element_type=F32)


def lane_ids(shape):
    return lax.broadcasted_iota(jnp.int32, shape, 1)


def from_below(values):
    return jnp.where(lane_ids(values.shape) == 0, 0.0, pltpu.roll(values, 1, 1))


def from_above(values):
    return jnp.where(
        lane_ids(values.shape) == LANES - 1, 0.0, pltpu.roll(values, LANES - 1, 1)
    )


def contribution_kernel(cells_ref, weight_ref, rest_ref, send_ref, square_ref, acc_ref, flat_ref):
    weight = weight_ref[...]
    acc_ref[...] = jnp.zeros_like(acc_ref)
    for x in range(4):
        for y in range(2):
            place = slice((x * 2 + y) * LANES, (x * 2 + y + 1) * LANES)
            flat_ref[:, place] = cells_ref[x, y]
        terms = dot_nn(weight, flat_ref[:, x * 256 : (x + 1) * 256])
        for e in range(3):
            for a in range(3):
                for b in range(3):
                    first = (9 * e + 3 * a + b) * 32
                    lanes = slice(b * LANES, (b + 2) * LANES)
                    acc_ref[e, x + a, :, lanes] = (
                        acc_ref[e, x + a, :, lanes] + terms[first : first + 32]
                    )
    for row in range(6):
        for y in range(4):
            lanes = slice(y * LANES, (y + 1) * LANES)
            total = (
                from_above(acc_ref[0, row, :, lanes])
                + acc_ref[1, row, :, lanes]
                + from_below(acc_ref[2, row, :, lanes])
            )
            if y < 2:
                rest_ref[row, y] = total
            else:
                send_ref[row, y - 2] = total
    cells = flat_ref[...]
    square_ref[...] = dot_nt(cells, cells)


def stacked_products(left_ref, stack_ref, out_ref):
    out_ref[:, 0:864] = dot_nt(left_ref[...], stack_ref[...])
    lower = stack_ref[96:288, :]
    first = dot_nt(lower, stack_ref[288:384, :])
    second = dot_nt(lower, stack_ref[576:672, :])
    out_ref[0:96, 864:960] = first[0:96]
    out_ref[0:96, 960:1056] = first[96:192]
    out_ref[0:96, 1056:1152] = second[0:96]
    out_ref[0:96, 1152:1248] = second[96:192]
    out_ref[0:96, 1248:1280] = jnp.zeros((96, 32), F32)


def chunk_pieces(tile, group):
    used = 960 // group
    first, last = 96 * tile, 96 * tile + 96
    for chunk in range(first // used, (last - 1) // used + 1):
        low, high = max(first, chunk * used), min(last, (chunk + 1) * used)
        yield low - first, high - low, chunk, low - chunk * used


def sums_kernel(
    group, core_ref, inner_ref, own_ref, outer_ref, back_ref, corner_ref, cells_ref, square_ref, weight_ref,
    keep_ref, send_ref,
    shifted_ref, hidden_ref, acc_ref, stack_one_ref, stack_two_ref,
    rows_one_ref, rows_two_ref, out_one_ref, out_two_ref,
):
    is_first = core_ref[0] == 0
    for x in range(8):
        for y in range(6):
            if 2 <= y < 4:
                column = own_ref[x, y - 2].astype(F32)
            else:
                inner = inner_ref[x, y % 2].astype(F32)
                outer = outer_ref[x, y % 2].astype(F32)
                column = jnp.where(is_first == (y < 2), outer, inner)
            lanes = slice((x * 6 + y) * LANES, (x * 6 + y + 1) * LANES)
            shifted_ref[0:32, lanes] = from_below(column).astype(BF16)
            shifted_ref[32:64, lanes] = column.astype(BF16)
            shifted_ref[64:96, lanes] = from_above(column).astype(BF16)
    weight = weight_ref[...]
    acc_ref[...] = jnp.zeros_like(acc_ref)
    for x in range(8):
        terms = dot_nn(weight, shifted_ref[:, x * 768 : (x + 1) * 768])
        for a in range(3):
            row = x - a + 1
            if 1 <= row <= 6:
                total = acc_ref[row - 1]
                for b in range(3):
                    first = (3 * a + b) * 32
                    total = total + terms[first : first + 32, b * LANES : b * LANES + 512]
                acc_ref[row - 1] = total
    for row in range(6):
        linear = acc_ref[row]
        logistic = 1.0 / (1.0 + jnp.exp(-linear))
        hidden = (linear * logistic).astype(BF16).astype(F32)
        for y in range(4):
            column = hidden[:, y * LANES : (y + 1) * LANES]
            lanes = slice((row * 4 + y) * LANES, (row * 4 + y + 1) * LANES)
            hidden_ref[0:32, lanes] = from_below(column).astype(BF16)
            hidden_ref[32:64, lanes] = column.astype(BF16)
            hidden_ref[64:96, lanes] = from_above(column).astype(BF16)
        if row < 4:
            slope = logistic * (1.0 + linear * (1.0 - logistic))
            for y in range(2):
                back = back_ref[row, y]
                if row < 2:
                    back = back + corner_ref[row, y]
                place = slice((row * 2 + y) * LANES, (row * 2 + y + 1) * LANES)
                signal = back * slope[:, y * LANES : (y + 1) * LANES]
                rows_one_ref[96:128, place] = signal.astype(BF16)
                rows_two_ref[96:224, place] = cells_ref[row, y]
    for a in range(3):
        for b in range(3):
            rows = slice((3 * a + b) * 96, (3 * a + b + 1) * 96)
            for x in range(4):
                lanes = slice(x * 256, (x + 1) * 256)
                one = ((x + a) * 6 + b) * LANES
                two = ((x + a) * 4 + b) * LANES
                stack_one_ref[rows, lanes] = shifted_ref[:, one : one + 256]
                stack_two_ref[rows, lanes] = hidden_ref[:, two : two + 256]
    rows_one_ref[0:96, :] = stack_one_ref[0:96, :]
    rows_two_ref[0:96, :] = stack_two_ref[0:96, :]
    stacked_products(rows_one_ref, stack_one_ref, out_one_ref)
    stacked_products(rows_two_ref, stack_two_ref, out_two_ref)
    signal = rows_one_ref[96:128, :]
    square_one = dot_nt(signal, signal)

    def put(rows, one, two):
        keep_ref[rows, :] = jnp.where(is_first, one, two)
        send_ref[rows, :] = jnp.where(is_first, two, one)

    height = ROWS // group
    keep_ref[0:ROWS, :] = jnp.zeros((ROWS, LANES), F32)
    send_ref[0:ROWS, :] = jnp.zeros((ROWS, LANES), F32)
    for tile in range(10):
        lanes = slice(tile * LANES, (tile + 1) * LANES)
        for row, count, chunk, place in chunk_pieces(tile, group):
            first = chunk * height + place
            put(
                slice(first, first + count),
                out_one_ref[row : row + count, lanes],
                out_two_ref[row : row + count, lanes],
            )
    nothing = jnp.zeros((96, LANES), F32)
    for tile in range(7):
        lanes = slice(tile * LANES, (tile + 1) * LANES)
        one = out_one_ref[96:128, lanes]
        two = out_two_ref[96:224, lanes]
        if tile == 6:
            one = jnp.where(lane_ids(one.shape) < 96, one, 0.0)
            two = jnp.where(lane_ids(two.shape) < 96, two, 0.0)
        put(
            slice(ROWS + tile * 128, ROWS + (tile + 1) * 128),
            jnp.concatenate([one, nothing], axis=0),
            two,
        )
    wide = jnp.concatenate([square_one, jnp.zeros((32, 96), F32)], axis=1)
    put(
        slice(ROWS + 896, ROWS + 1024), jnp.concatenate([wide, nothing], axis=0), square_ref[...]
    )


def split_rows(values):
    high = values.astype(BF16)
    low = (values - high.astype(F32)).astype(BF16)
    return jnp.concatenate([high, low], axis=0)


LN2 = math.log(2.0)


def power_of(values):
    largest = jnp.max(jnp.max(jnp.abs(values), axis=0, keepdims=True), axis=1, keepdims=True)
    return jnp.ceil(jnp.log(jnp.maximum(largest, 1e-30)) * (1.0 / LN2)) - 14.0


def two_to(power):
    return jnp.exp(power * LN2)


def pack_kernel(keep_ref, other_ref, out_ref):
    group, _, height, _ = out_ref.shape
    used = 960 // group
    plain = 896 // height
    edge = ROWS + plain * height
    for section, first, last, low, high in (
        (0, 0, ROWS, 0, group),
        (1, ROWS, edge, 0, plain),
        (1, edge, 2 * ROWS, plain, group),
    ):
        values = keep_ref[first:last, :] + other_ref[first:last, :]
        power = power_of(values)
        values = (values * two_to(-power)).reshape(high - low, height, LANES)
        out_ref[low:high, section] = values
        if section == 0:
            corr_power = power
        else:
            out_ref[low:high, 0, used + 1 : used + 2, :] = jnp.broadcast_to(
                power.reshape(1, 1, 1), (high - low, 1, LANES)
            )
    out_ref[:, 0, used : used + 1, :] = jnp.broadcast_to(
        corr_power.reshape(1, 1, 1), (group, 1, LANES)
    )


def opened(parts_ref, group):
    used = 960 // group
    powers = parts_ref[:, 0]
    corr = powers * two_to(powers[:, used : used + 1])
    rows = lax.broadcasted_iota(jnp.int32, corr.shape, 1)
    corr = jnp.where(rows < used, corr, 0.0)
    grad = parts_ref[:, 1] * two_to(powers[:, used + 1 : used + 2])
    return corr, grad


def total_kernel(parts_ref, out_ref):
    corr, grad = opened(parts_ref, parts_ref.shape[0])
    corr, grad = jnp.sum(corr, axis=0), jnp.sum(grad, axis=0)
    high = grad.astype(BF16)
    out_ref[0] = corr.astype(BF16)
    out_ref[1] = high
    out_ref[2] = (grad - high.astype(F32)).astype(BF16)


def deep_kernel(group, parts_ref, out_ref):
    used = 960 // group
    parts = parts_ref[...].astype(F32)
    corr = jnp.sum(parts[:, 0], axis=0)
    grad = jnp.sum(parts[:, 1] + parts[:, 2], axis=0)
    for section, values in ((0, corr), (1, grad)):
        power = power_of(values)
        out_ref[section] = values * two_to(-power)
        if section == 0:
            corr_power = power
        else:
            out_ref[0, used + 1 : used + 2, :] = jnp.broadcast_to(power, (1, LANES))
    out_ref[0, used : used + 1, :] = jnp.broadcast_to(corr_power, (1, LANES))


def small_call(kernel, name, shape, dtype, *arrays):
    return pl.pallas_call(
        kernel,
        out_shape=jax.ShapeDtypeStruct(shape, dtype),
        in_specs=in_vmem(len(arrays)),
        out_specs=in_vmem(1)[0],
        compiler_params=params(),
        name=name,
    )(*arrays)


def root_kernel(total_cells, core_ref, sums_ref, order_ref, out_ref, strip_ref, full_ref, factor_ref):
    group = sums_ref.shape[0]
    parts, grads = opened(sums_ref, group)
    grads = grads.reshape(ROWS, LANES)
    tiles = []
    for tile in range(10):
        pieces = [
            parts[chunk, place : place + count]
            for _, count, chunk, place in chunk_pieces(tile, group)
        ]
        tiles.append(jnp.concatenate(pieces, axis=0))
    corr = jnp.concatenate(tiles, axis=1)
    gradient = jnp.concatenate([grads[128 * j : 128 * j + 128] for j in range(7)], axis=1)[:, 0:864]

    def identity(order, dtype):
        rows = lax.broadcasted_iota(jnp.int32, (order, order), 0)
        return jnp.where(rows == lane_ids((order, order)), 1.0, 0.0).astype(dtype)

    eye_96 = identity(96, BF16)
    eye_288 = identity(288, BF16)
    strip_ref[0, :, 0:96] = dot_nt(eye_96, corr[:, 192:288].astype(BF16))
    strip_ref[0, :, 96:192] = dot_nt(eye_96, corr[:, 96:192].astype(BF16))
    strip_ref[0, :, 192:480] = corr[:, 0:288]
    strip_ref[1, :, 0:96] = corr[:, 960:1056]
    strip_ref[1, :, 96:192] = corr[:, 864:960]
    strip_ref[1, :, 192:480] = corr[:, 288:576]
    strip_ref[2, :, 0:96] = corr[:, 1152:1248]
    strip_ref[2, :, 96:192] = corr[:, 1056:1152]
    strip_ref[2, :, 192:480] = corr[:, 576:864]
    for b in range(3):
        for step in range(3):
            piece = strip_ref[step, :, (2 - b) * 96 : (2 - b) * 96 + 288]
            for a in range(3 - step):
                first = a * 288 + b * 96
                full_ref[first : first + 96, (a + step) * 288 : (a + step + 1) * 288] = piece
    turned_one = dot_nt(eye_288, full_ref[0:288, 288:576].astype(BF16))
    turned_two = dot_nt(eye_288, full_ref[0:288, 576:864].astype(BF16))
    full_ref[288:576, 0:288] = turned_one
    full_ref[576:864, 288:576] = turned_one
    full_ref[576:864, 0:288] = turned_two
    whole = full_ref[...]
    factor_ref[...] = whole.astype(BF16)
    bound = jnp.max(jnp.sum(jnp.abs(whole), axis=0, keepdims=True)) / total_cells + DAMPING
    scale = 1.0 / (bound * total_cells)
    shift = DAMPING / bound

    def times(rows):
        product = dot_nn(split_rows(rows), factor_ref[...])
        return (product[0:128] + product[128:256]) * scale + rows * shift

    def once(rows):
        return 1.5 * rows - 0.5 * times(rows)

    def iterate(rows, step):
        if step == 0:
            return once(rows)
        first = iterate(rows, step - 1)
        second = iterate(iterate(times(first), step - 1), step - 1)
        return 1.5 * first - 0.5 * second

    right = iterate(gradient, ITERS - 1)

    eye_128 = identity(128, F32)
    small = grads[896:1024] / total_cells + DAMPING * eye_128
    small_bound = jnp.max(jnp.sum(jnp.abs(small), axis=0, keepdims=True))
    scaled = small / small_bound
    root = 1.5 * eye_128 - 0.5 * scaled
    for _ in range(ITERS - 1):
        product = square_product(square_product(square_product(root, scaled), root), root)
        root = 1.5 * root - 0.5 * product
    factor = 1.0 / (math.sqrt(total_cells) * jnp.sqrt(small_bound) * jnp.sqrt(bound))
    both = split_rows(root)
    high = right.astype(BF16)
    low = (right - high.astype(F32)).astype(BF16)
    update = dot_nn(both, high)
    update = (update[0:128] + update[128:256] + dot_nn(both[0:128], low)) * factor
    ordered = dot_nn(split_rows(update), order_ref[...])
    ordered = ordered[0:128] + ordered[128:256]
    ordered = jnp.concatenate([ordered, jnp.zeros((128, 32), F32)], axis=1)
    is_first = core_ref[0] == 0
    for tile in range(7):
        piece = ordered[:, tile * LANES : (tile + 1) * LANES]
        turned = piece.T
        out_ref[tile * 128 : min(tile * 128 + 128, 864), :] = turned[0 : min(128, 864 - tile * 128)]

    @pl.when(is_first)
    def _():
        for tile in range(7):
            out_ref[tile * 32 : tile * 32 + 32, :] = ordered[
                0:32, tile * LANES : (tile + 1) * LANES
            ]


def square_product(left, right):
    high = right.astype(BF16)
    low = (right - high.astype(F32)).astype(BF16)
    product = dot_nn(split_rows(left), jnp.concatenate([high, low], axis=1))
    return product[0:128, 0:128] + product[0:128, 128:256] + product[128:256, 0:128]


def pick_kernel(core_ref, mine_ref, other_ref, one_ref, two_ref):
    is_first = core_ref[0] == 0
    for tile in range(7):
        rows = slice(tile * 32, tile * 32 + 32)
        piece = jnp.where(is_first, mine_ref[rows, :], other_ref[rows, :])
        width = min(LANES, 864 - tile * LANES)
        one_ref[:, tile * LANES : tile * LANES + width] = piece[:, 0:width]
    two_ref[...] = jnp.where(is_first, other_ref[...], mine_ref[...])


def plane_order():
    order = np.zeros((864, 864), np.float32)
    for offset in range(27):
        for channel in range(32):
            order[offset * 32 + channel, channel * 27 + offset] = 1.0
    return jnp.asarray(order, BF16)


def params():
    return pltpu.CompilerParams(vmem_limit_bytes=VMEM_LIMIT)


def in_vmem(count):
    return [pl.BlockSpec(memory_space=pltpu.VMEM)] * count


def contributions(cells, weight):
    shape = jax.ShapeDtypeStruct
    return pl.pallas_call(
        contribution_kernel,
        out_shape=(
            shape((6, 2, 32, LANES), F32),
            shape((6, 2, 32, LANES), F32),
            shape((128, 128), F32),
        ),
        in_specs=in_vmem(2),
        out_specs=tuple(in_vmem(3)),
        scratch_shapes=[pltpu.VMEM((3, 6, 32, 512), F32), pltpu.VMEM((128, 1024), BF16)],
        compiler_params=params(),
        cost_estimate=pl.CostEstimate(
            flops=300_000_000, bytes_accessed=2_000_000, transcendentals=0
        ),
        name="contributions",
    )(cells, weight)


def sums(group, core, left, own, right, back, corner, cells, square, weight):
    shape = jax.ShapeDtypeStruct
    return pl.pallas_call(
        functools.partial(sums_kernel, group),
        out_shape=(shape((2 * ROWS, LANES), F32), shape((2 * ROWS, LANES), F32)),
        in_specs=[pl.BlockSpec(memory_space=pltpu.SMEM)] + in_vmem(8),
        out_specs=tuple(in_vmem(2)),
        scratch_shapes=[
            pltpu.VMEM((96, 6144), BF16),
            pltpu.VMEM((96, 3072), BF16),
            pltpu.VMEM((6, 32, 512), F32),
            pltpu.VMEM((864, 1024), BF16),
            pltpu.VMEM((864, 1024), BF16),
            pltpu.VMEM((128, 1024), BF16),
            pltpu.VMEM((224, 1024), BF16),
            pltpu.VMEM((128, 1280), F32),
            pltpu.VMEM((224, 1280), F32),
        ],
        compiler_params=params(),
        cost_estimate=pl.CostEstimate(
            flops=3_000_000_000, bytes_accessed=6_000_000, transcendentals=200_000
        ),
        name="sums",
    )(core, left, own, right, back, corner, cells, square, weight)


def updates(total_cells, core, sums, order):
    return pl.pallas_call(
        functools.partial(root_kernel, total_cells),
        out_shape=jax.ShapeDtypeStruct((864, 128), F32),
        in_specs=[pl.BlockSpec(memory_space=pltpu.SMEM)] + in_vmem(2),
        out_specs=in_vmem(1)[0],
        scratch_shapes=[
            pltpu.VMEM((3, 96, 512), F32),
            pltpu.VMEM((864, 864), F32),
            pltpu.VMEM((864, 864), BF16),
        ],
        compiler_params=params(),
        cost_estimate=pl.CostEstimate(
            flops=8_000_000_000, bytes_accessed=6_000_000, transcendentals=1000
        ),
        name="updates",
    )(core, sums, order)


def picked(core, mine, other):
    shape = jax.ShapeDtypeStruct
    return pl.pallas_call(
        pick_kernel,
        out_shape=(shape((32, 864), F32), shape((864, 128), F32)),
        in_specs=[pl.BlockSpec(memory_space=pltpu.SMEM)] + in_vmem(2),
        compiler_params=params(),
        name="picked",
    )(core, mine, other)


def pairs(count, offset):
    return [(i, (i + 1 if (i - offset) % 2 == 0 else i - 1) % count) for i in range(count)]


def on_device(density, weight_one, weight_two, cotangent):
    grid_x = lax.axis_size("y") * lax.axis_size("zh")
    grid_y = lax.axis_size("gc") * lax.axis_size("core")
    total_cells = 1024 * grid_x * grid_y
    core = lax.axis_index("core").astype(jnp.int32).reshape(1)

    def from_x(block, distance):
        pairs = [((i + distance) % grid_x, i) for i in range(grid_x)]
        return lax.ppermute(block, ("y", "zh"), pairs)

    def from_y(block, distance):
        pairs = [((i + distance) % grid_y, i) for i in range(grid_y)]
        return lax.ppermute(block, ("gc", "core"), pairs)

    def other_core(block):
        return lax.ppermute(block, "core", [(0, 1), (1, 0)])

    field = density.transpose(1, 2, 0, 3)
    low, high = field[0:2], field[2:4]
    even = lax.axis_index("zh") % 2 == 0
    first = lax.ppermute(jnp.where(even, high, low), ("y", "zh"), pairs(grid_x, 0))
    second = lax.ppermute(jnp.where(even, low, high), ("y", "zh"), pairs(grid_x, 1))
    field = jnp.concatenate(
        [jnp.where(even, second, first), field, jnp.where(even, first, second)], axis=0
    )
    inner = other_core(field)
    outer = lax.ppermute(field, ("gc", "core"), pairs(grid_y, 1))
    cells = cotangent.transpose(1, 2, 0, 3)
    kernel_one = weight_one.reshape(32, 32, 3, 3, 3).transpose(2, 3, 0, 4, 1).reshape(288, 96)
    kernel_two = weight_two.reshape(128, 32, 3, 3, 3).transpose(4, 2, 3, 1, 0).reshape(864, 128)
    back, beyond, square = contributions(cells, kernel_two)
    back = back + from_y(beyond, -1)
    corner = from_x(back[4:6], -1)
    group = lax.axis_size("y") * lax.axis_size("gc")
    keep, send = sums(group, core, inner, field, outer, back[0:4], corner, cells, square, kernel_one)
    height = ROWS // group
    deep = lax.axis_size("zh")

    def exchanged(parts, axes):
        return lax.all_to_all(parts, axes, 0, 0, tiled=True)

    def narrow(parts):
        return parts.astype(jnp.float16)

    parts = small_call(
        pack_kernel, "pack", (group, 2, height, LANES), F32, keep, other_core(send)
    )
    parts = exchanged(narrow(parts), ("y", "gc")).astype(F32)
    own = small_call(total_kernel, "total", (3, height, LANES), BF16, parts)
    own = exchanged(jnp.broadcast_to(own[None], (deep,) + own.shape), "zh")
    own = small_call(
        functools.partial(deep_kernel, group), "deep", (2, height, LANES), F32, own
    )
    own = jnp.broadcast_to(narrow(own)[None], (group,) + own.shape)
    gathered = exchanged(own, ("y", "gc")).astype(F32)
    mine = updates(float(total_cells), core, gathered, plane_order())
    update_one, update_two = picked(core, mine, other_core(mine))
    return (update_one, update_two.T)


def solution(mesh):
    grid_x, grid_y = mesh.shape["gx"], mesh.shape["gy"]
    deep = max(grid_x // 4, 2)
    inner = Mesh(
        mesh.devices.reshape(grid_x // deep, deep, grid_y // 2, 2), ("y", "zh", "gc", "core")
    )
    split = P(None, ("y", "zh"), ("gc", "core"), None)
    return jax.shard_map(
        on_device,
        mesh=inner,
        in_specs=(split, P(), P(), split),
        out_specs=(P(), P()),
        check_vma=False,
    )
```

```python
import functools
import math

import jax
import jax.numpy as jnp
import numpy as np
from jax import lax
from jax.experimental import pallas as pl
from jax.experimental.pallas import tpu as pltpu
from jax.sharding import Mesh, PartitionSpec as P

ITERS = 3
DAMPING = 0.1
F32 = jnp.float32
BF16 = jnp.bfloat16
VMEM_LIMIT = 20 * 1024 * 1024
ROWS = 1024
LANES = 128


def dot_nt(left, right):
    return lax.dot_general(left, right, (((1,), (1,)), ((), ())), preferred_element_type=F32)


def dot_nn(left, right):
    return jnp.dot(left, right, preferred_element_type=F32)


def lane_ids(shape):
    return lax.broadcasted_iota(jnp.int32, shape, 1)


def from_below(values):
    return jnp.where(lane_ids(values.shape) == 0, 0.0, pltpu.roll(values, 1, 1))


def from_above(values):
    return jnp.where(
        lane_ids(values.shape) == LANES - 1, 0.0, pltpu.roll(values, LANES - 1, 1)
    )


def contribution_kernel(cells_ref, weight_ref, rest_ref, send_ref, square_ref, acc_ref, flat_ref):
    weight = weight_ref[...]
    acc_ref[...] = jnp.zeros_like(acc_ref)
    for x in range(4):
        for y in range(2):
            place = slice((x * 2 + y) * LANES, (x * 2 + y + 1) * LANES)
            flat_ref[:, place] = cells_ref[x, y]
        terms = dot_nn(weight, flat_ref[:, x * 256 : (x + 1) * 256])
        for e in range(3):
            for a in range(3):
                for b in range(3):
                    first = (9 * e + 3 * a + b) * 32
                    lanes = slice(b * LANES, (b + 2) * LANES)
                    acc_ref[e, x + a, :, lanes] = (
                        acc_ref[e, x + a, :, lanes] + terms[first : first + 32]
                    )
    for row in range(6):
        for y in range(4):
            lanes = slice(y * LANES, (y + 1) * LANES)
            total = (
                from_above(acc_ref[0, row, :, lanes])
                + acc_ref[1, row, :, lanes]
                + from_below(acc_ref[2, row, :, lanes])
            )
            if y < 2:
                rest_ref[row, y] = total
            else:
                send_ref[row, y - 2] = total
    cells = flat_ref[...]
    square_ref[...] = dot_nt(cells, cells)


def stacked_products(left_ref, stack_ref, out_ref):
    out_ref[:, 0:864] = dot_nt(left_ref[...], stack_ref[...])
    lower = stack_ref[96:288, :]
    first = dot_nt(lower, stack_ref[288:384, :])
    second = dot_nt(lower, stack_ref[576:672, :])
    out_ref[0:96, 864:960] = first[0:96]
    out_ref[0:96, 960:1056] = first[96:192]
    out_ref[0:96, 1056:1152] = second[0:96]
    out_ref[0:96, 1152:1248] = second[96:192]
    out_ref[0:96, 1248:1280] = jnp.zeros((96, 32), F32)


def chunk_pieces(tile, group):
    used = 960 // group
    first, last = 96 * tile, 96 * tile + 96
    for chunk in range(first // used, (last - 1) // used + 1):
        low, high = max(first, chunk * used), min(last, (chunk + 1) * used)
        yield low - first, high - low, chunk, low - chunk * used


def sums_kernel(
    group, core_ref, inner_ref, own_ref, outer_ref, back_ref, corner_ref, cells_ref, square_ref, weight_ref,
    keep_ref, send_ref,
    shifted_ref, hidden_ref, acc_ref, stack_one_ref, stack_two_ref,
    rows_one_ref, rows_two_ref, out_one_ref, out_two_ref,
):
    is_first = core_ref[0] == 0
    for x in range(8):
        for y in range(6):
            if 2 <= y < 4:
                column = own_ref[x, y - 2].astype(F32)
            else:
                inner = inner_ref[x, y % 2].astype(F32)
                outer = outer_ref[x, y % 2].astype(F32)
                column = jnp.where(is_first == (y < 2), outer, inner)
            lanes = slice((x * 6 + y) * LANES, (x * 6 + y + 1) * LANES)
            shifted_ref[0:32, lanes] = from_below(column).astype(BF16)
            shifted_ref[32:64, lanes] = column.astype(BF16)
            shifted_ref[64:96, lanes] = from_above(column).astype(BF16)
    weight = weight_ref[...]
    acc_ref[...] = jnp.zeros_like(acc_ref)
    for x in range(8):
        terms = dot_nn(weight, shifted_ref[:, x * 768 : (x + 1) * 768])
        for a in range(3):
            row = x - a + 1
            if 1 <= row <= 6:
                total = acc_ref[row - 1]
                for b in range(3):
                    first = (3 * a + b) * 32
                    total = total + terms[first : first + 32, b * LANES : b * LANES + 512]
                acc_ref[row - 1] = total
    for row in range(6):
        linear = acc_ref[row]
        logistic = 1.0 / (1.0 + jnp.exp(-linear))
        hidden = (linear * logistic).astype(BF16).astype(F32)
        for y in range(4):
            column = hidden[:, y * LANES : (y + 1) * LANES]
            lanes = slice((row * 4 + y) * LANES, (row * 4 + y + 1) * LANES)
            hidden_ref[0:32, lanes] = from_below(column).astype(BF16)
            hidden_ref[32:64, lanes] = column.astype(BF16)
            hidden_ref[64:96, lanes] = from_above(column).astype(BF16)
        if row < 4:
            slope = logistic * (1.0 + linear * (1.0 - logistic))
            for y in range(2):
                back = back_ref[row, y]
                if row < 2:
                    back = back + corner_ref[row, y]
                place = slice((row * 2 + y) * LANES, (row * 2 + y + 1) * LANES)
                signal = back * slope[:, y * LANES : (y + 1) * LANES]
                rows_one_ref[96:128, place] = signal.astype(BF16)
                rows_two_ref[96:224, place] = cells_ref[row, y]
    for a in range(3):
        for b in range(3):
            rows = slice((3 * a + b) * 96, (3 * a + b + 1) * 96)
            for x in range(4):
                lanes = slice(x * 256, (x + 1) * 256)
                one = ((x + a) * 6 + b) * LANES
                two = ((x + a) * 4 + b) * LANES
                stack_one_ref[rows, lanes] = shifted_ref[:, one : one + 256]
                stack_two_ref[rows, lanes] = hidden_ref[:, two : two + 256]
    rows_one_ref[0:96, :] = stack_one_ref[0:96, :]
    rows_two_ref[0:96, :] = stack_two_ref[0:96, :]
    stacked_products(rows_one_ref, stack_one_ref, out_one_ref)
    stacked_products(rows_two_ref, stack_two_ref, out_two_ref)
    signal = rows_one_ref[96:128, :]
    square_one = dot_nt(signal, signal)

    def put(rows, one, two):
        keep_ref[rows, :] = jnp.where(is_first, one, two)
        send_ref[rows, :] = jnp.where(is_first, two, one)

    height = ROWS // group
    keep_ref[0:ROWS, :] = jnp.zeros((ROWS, LANES), F32)
    send_ref[0:ROWS, :] = jnp.zeros((ROWS, LANES), F32)
    for tile in range(10):
        lanes = slice(tile * LANES, (tile + 1) * LANES)
        for row, count, chunk, place in chunk_pieces(tile, group):
            first = chunk * height + place
            put(
                slice(first, first + count),
                out_one_ref[row : row + count, lanes],
                out_two_ref[row : row + count, lanes],
            )
    nothing = jnp.zeros((96, LANES), F32)
    for tile in range(7):
        lanes = slice(tile * LANES, (tile + 1) * LANES)
        one = out_one_ref[96:128, lanes]
        two = out_two_ref[96:224, lanes]
        if tile == 6:
            one = jnp.where(lane_ids(one.shape) < 96, one, 0.0)
            two = jnp.where(lane_ids(two.shape) < 96, two, 0.0)
        put(
            slice(ROWS + tile * 128, ROWS + (tile + 1) * 128),
            jnp.concatenate([one, nothing], axis=0),
            two,
        )
    wide = jnp.concatenate([square_one, jnp.zeros((32, 96), F32)], axis=1)
    put(
        slice(ROWS + 896, ROWS + 1024), jnp.concatenate([wide, nothing], axis=0), square_ref[...]
    )


def split_rows(values):
    high = values.astype(BF16)
    low = (values - high.astype(F32)).astype(BF16)
    return jnp.concatenate([high, low], axis=0)


LN2 = math.log(2.0)


def power_of(values):
    largest = jnp.max(jnp.max(jnp.abs(values), axis=0, keepdims=True), axis=1, keepdims=True)
    return jnp.ceil(jnp.log(jnp.maximum(largest, 1e-30)) * (1.0 / LN2)) - 14.0


def two_to(power):
    return jnp.exp(power * LN2)


def pack_kernel(keep_ref, corr_ref, grad_ref, out_ref):
    group, _, height, _ = out_ref.shape
    used = 960 // group
    plain = 896 // height
    edge = ROWS + plain * height
    for section, first, last, low, high in (
        (0, 0, ROWS, 0, group),
        (1, ROWS, edge, 0, plain),
        (1, edge, 2 * ROWS, plain, group),
    ):
        if section == 0:
            other = corr_ref[...].astype(F32)
        else:
            other = grad_ref[first - ROWS : last - ROWS, :]
        values = keep_ref[first:last, :] + other
        power = power_of(values)
        values = (values * two_to(-power)).reshape(high - low, height, LANES)
        out_ref[low:high, section] = values
        if section == 0:
            corr_power = power
        else:
            out_ref[low:high, 0, used + 1 : used + 2, :] = jnp.broadcast_to(
                power.reshape(1, 1, 1), (high - low, 1, LANES)
            )
    out_ref[:, 0, used : used + 1, :] = jnp.broadcast_to(
        corr_power.reshape(1, 1, 1), (group, 1, LANES)
    )


def opened(parts_ref, group):
    used = 960 // group
    powers = parts_ref[:, 0]
    corr = powers * two_to(powers[:, used : used + 1])
    rows = lax.broadcasted_iota(jnp.int32, corr.shape, 1)
    corr = jnp.where(rows < used, corr, 0.0)
    grad = parts_ref[:, 1] * two_to(powers[:, used + 1 : used + 2])
    return corr, grad


def total_kernel(parts_ref, out_ref):
    corr, grad = opened(parts_ref, parts_ref.shape[0])
    corr, grad = jnp.sum(corr, axis=0), jnp.sum(grad, axis=0)
    high = grad.astype(BF16)
    out_ref[0] = corr.astype(BF16)
    out_ref[1] = high
    out_ref[2] = (grad - high.astype(F32)).astype(BF16)


def deep_kernel(group, parts_ref, out_ref):
    used = 960 // group
    parts = parts_ref[...].astype(F32)
    corr = jnp.sum(parts[:, 0], axis=0)
    grad = jnp.sum(parts[:, 1] + parts[:, 2], axis=0)
    for section, values in ((0, corr), (1, grad)):
        power = power_of(values)
        out_ref[section] = values * two_to(-power)
        if section == 0:
            corr_power = power
        else:
            out_ref[0, used + 1 : used + 2, :] = jnp.broadcast_to(power, (1, LANES))
    out_ref[0, used : used + 1, :] = jnp.broadcast_to(corr_power, (1, LANES))


def small_call(kernel, name, shape, dtype, *arrays):
    return pl.pallas_call(
        kernel,
        out_shape=jax.ShapeDtypeStruct(shape, dtype),
        in_specs=in_vmem(len(arrays)),
        out_specs=in_vmem(1)[0],
        compiler_params=params(),
        name=name,
    )(*arrays)


def root_kernel(total_cells, core_ref, sums_ref, order_ref, out_ref, strip_ref, full_ref, factor_ref):
    group = sums_ref.shape[0]
    parts, grads = opened(sums_ref, group)
    grads = grads.reshape(ROWS, LANES)
    tiles = []
    for tile in range(10):
        pieces = [
            parts[chunk, place : place + count]
            for _, count, chunk, place in chunk_pieces(tile, group)
        ]
        tiles.append(jnp.concatenate(pieces, axis=0))
    corr = jnp.concatenate(tiles, axis=1)
    gradient = jnp.concatenate([grads[128 * j : 128 * j + 128] for j in range(7)], axis=1)[:, 0:864]

    def identity(order, dtype):
        rows = lax.broadcasted_iota(jnp.int32, (order, order), 0)
        return jnp.where(rows == lane_ids((order, order)), 1.0, 0.0).astype(dtype)

    eye_96 = identity(96, BF16)
    eye_288 = identity(288, BF16)
    strip_ref[0, :, 0:96] = dot_nt(eye_96, corr[:, 192:288].astype(BF16))
    strip_ref[0, :, 96:192] = dot_nt(eye_96, corr[:, 96:192].astype(BF16))
    strip_ref[0, :, 192:480] = corr[:, 0:288]
    strip_ref[1, :, 0:96] = corr[:, 960:1056]
    strip_ref[1, :, 96:192] = corr[:, 864:960]
    strip_ref[1, :, 192:480] = corr[:, 288:576]
    strip_ref[2, :, 0:96] = corr[:, 1152:1248]
    strip_ref[2, :, 96:192] = corr[:, 1056:1152]
    strip_ref[2, :, 192:480] = corr[:, 576:864]
    for b in range(3):
        for step in range(3):
            piece = strip_ref[step, :, (2 - b) * 96 : (2 - b) * 96 + 288]
            for a in range(3 - step):
                first = a * 288 + b * 96
                full_ref[first : first + 96, (a + step) * 288 : (a + step + 1) * 288] = piece
    turned_one = dot_nt(eye_288, full_ref[0:288, 288:576].astype(BF16))
    turned_two = dot_nt(eye_288, full_ref[0:288, 576:864].astype(BF16))
    full_ref[288:576, 0:288] = turned_one
    full_ref[576:864, 288:576] = turned_one
    full_ref[576:864, 0:288] = turned_two
    whole = full_ref[...]
    factor_ref[...] = whole.astype(BF16)
    bound = jnp.max(jnp.sum(jnp.abs(whole), axis=0, keepdims=True)) / total_cells + DAMPING
    scale = 1.0 / (bound * total_cells)
    shift = DAMPING / bound

    def times(rows):
        product = dot_nn(split_rows(rows), factor_ref[...])
        return (product[0:128] + product[128:256]) * scale + rows * shift

    def once(rows):
        return 1.5 * rows - 0.5 * times(rows)

    def iterate(rows, step):
        if step == 0:
            return once(rows)
        first = iterate(rows, step - 1)
        second = iterate(iterate(times(first), step - 1), step - 1)
        return 1.5 * first - 0.5 * second

    right = iterate(gradient, ITERS - 1)

    eye_128 = identity(128, F32)
    small = grads[896:1024] / total_cells + DAMPING * eye_128
    small_bound = jnp.max(jnp.sum(jnp.abs(small), axis=0, keepdims=True))
    scaled = small / small_bound
    root = 1.5 * eye_128 - 0.5 * scaled
    for _ in range(ITERS - 1):
        product = square_product(square_product(square_product(root, scaled), root), root)
        root = 1.5 * root - 0.5 * product
    factor = 1.0 / (math.sqrt(total_cells) * jnp.sqrt(small_bound) * jnp.sqrt(bound))
    both = split_rows(root)
    high = right.astype(BF16)
    low = (right - high.astype(F32)).astype(BF16)
    update = dot_nn(both, high)
    update = (update[0:128] + update[128:256] + dot_nn(both[0:128], low)) * factor
    ordered = dot_nn(split_rows(update), order_ref[...])
    ordered = ordered[0:128] + ordered[128:256]
    ordered = jnp.concatenate([ordered, jnp.zeros((128, 32), F32)], axis=1)
    is_first = core_ref[0] == 0
    for tile in range(7):
        piece = ordered[:, tile * LANES : (tile + 1) * LANES]
        turned = piece.T
        out_ref[tile * 128 : min(tile * 128 + 128, 864), :] = turned[0 : min(128, 864 - tile * 128)]

    @pl.when(is_first)
    def _():
        for tile in range(7):
            out_ref[tile * 32 : tile * 32 + 32, :] = ordered[
                0:32, tile * LANES : (tile + 1) * LANES
            ]


def square_product(left, right):
    high = right.astype(BF16)
    low = (right - high.astype(F32)).astype(BF16)
    product = dot_nn(split_rows(left), jnp.concatenate([high, low], axis=1))
    return product[0:128, 0:128] + product[0:128, 128:256] + product[128:256, 0:128]


def pick_kernel(core_ref, mine_ref, other_ref, one_ref, two_ref):
    is_first = core_ref[0] == 0
    for tile in range(7):
        rows = slice(tile * 32, tile * 32 + 32)
        piece = jnp.where(is_first, mine_ref[rows, :], other_ref[rows, :])
        width = min(LANES, 864 - tile * LANES)
        one_ref[:, tile * LANES : tile * LANES + width] = piece[:, 0:width]
    two_ref[...] = jnp.where(is_first, other_ref[...], mine_ref[...])


def plane_order():
    order = np.zeros((864, 864), np.float32)
    for offset in range(27):
        for channel in range(32):
            order[offset * 32 + channel, channel * 27 + offset] = 1.0
    return jnp.asarray(order, BF16)


def params():
    return pltpu.CompilerParams(vmem_limit_bytes=VMEM_LIMIT)


def in_vmem(count):
    return [pl.BlockSpec(memory_space=pltpu.VMEM)] * count


def contributions(cells, weight):
    shape = jax.ShapeDtypeStruct
    return pl.pallas_call(
        contribution_kernel,
        out_shape=(
            shape((6, 2, 32, LANES), F32),
            shape((6, 2, 32, LANES), F32),
            shape((128, 128), F32),
        ),
        in_specs=in_vmem(2),
        out_specs=tuple(in_vmem(3)),
        scratch_shapes=[pltpu.VMEM((3, 6, 32, 512), F32), pltpu.VMEM((128, 1024), BF16)],
        compiler_params=params(),
        cost_estimate=pl.CostEstimate(
            flops=300_000_000, bytes_accessed=2_000_000, transcendentals=0
        ),
        name="contributions",
    )(cells, weight)


def sums(group, core, left, own, right, back, corner, cells, square, weight):
    shape = jax.ShapeDtypeStruct
    return pl.pallas_call(
        functools.partial(sums_kernel, group),
        out_shape=(shape((2 * ROWS, LANES), F32), shape((2 * ROWS, LANES), F32)),
        in_specs=[pl.BlockSpec(memory_space=pltpu.SMEM)] + in_vmem(8),
        out_specs=tuple(in_vmem(2)),
        scratch_shapes=[
            pltpu.VMEM((96, 6144), BF16),
            pltpu.VMEM((96, 3072), BF16),
            pltpu.VMEM((6, 32, 512), F32),
            pltpu.VMEM((864, 1024), BF16),
            pltpu.VMEM((864, 1024), BF16),
            pltpu.VMEM((128, 1024), BF16),
            pltpu.VMEM((224, 1024), BF16),
            pltpu.VMEM((128, 1280), F32),
            pltpu.VMEM((224, 1280), F32),
        ],
        compiler_params=params(),
        cost_estimate=pl.CostEstimate(
            flops=3_000_000_000, bytes_accessed=6_000_000, transcendentals=200_000
        ),
        name="sums",
    )(core, left, own, right, back, corner, cells, square, weight)


def updates(total_cells, core, sums, order):
    return pl.pallas_call(
        functools.partial(root_kernel, total_cells),
        out_shape=jax.ShapeDtypeStruct((864, 128), F32),
        in_specs=[pl.BlockSpec(memory_space=pltpu.SMEM)] + in_vmem(2),
        out_specs=in_vmem(1)[0],
        scratch_shapes=[
            pltpu.VMEM((3, 96, 512), F32),
            pltpu.VMEM((864, 864), F32),
            pltpu.VMEM((864, 864), BF16),
        ],
        compiler_params=params(),
        cost_estimate=pl.CostEstimate(
            flops=8_000_000_000, bytes_accessed=6_000_000, transcendentals=1000
        ),
        name="updates",
    )(core, sums, order)


def picked(core, mine, other):
    shape = jax.ShapeDtypeStruct
    return pl.pallas_call(
        pick_kernel,
        out_shape=(shape((32, 864), F32), shape((864, 128), F32)),
        in_specs=[pl.BlockSpec(memory_space=pltpu.SMEM)] + in_vmem(2),
        compiler_params=params(),
        name="picked",
    )(core, mine, other)


def pairs(count, offset):
    return [(i, (i + 1 if (i - offset) % 2 == 0 else i - 1) % count) for i in range(count)]


def on_device(density, weight_one, weight_two, cotangent):
    grid_x = lax.axis_size("y") * lax.axis_size("zh")
    grid_y = lax.axis_size("gc") * lax.axis_size("core")
    total_cells = 1024 * grid_x * grid_y
    core = lax.axis_index("core").astype(jnp.int32).reshape(1)

    def from_x(block, distance):
        pairs = [((i + distance) % grid_x, i) for i in range(grid_x)]
        return lax.ppermute(block, ("y", "zh"), pairs)

    def from_y(block, distance):
        pairs = [((i + distance) % grid_y, i) for i in range(grid_y)]
        return lax.ppermute(block, ("gc", "core"), pairs)

    def other_core(block):
        return lax.ppermute(block, "core", [(0, 1), (1, 0)])

    field = density.transpose(1, 2, 0, 3)
    low, high = field[0:2], field[2:4]
    even = lax.axis_index("zh") % 2 == 0
    first = lax.ppermute(jnp.where(even, high, low), ("y", "zh"), pairs(grid_x, 0))
    second = lax.ppermute(jnp.where(even, low, high), ("y", "zh"), pairs(grid_x, 1))
    field = jnp.concatenate(
        [jnp.where(even, second, first), field, jnp.where(even, first, second)], axis=0
    )
    inner = other_core(field)
    outer = lax.ppermute(field, ("gc", "core"), pairs(grid_y, 1))
    cells = cotangent.transpose(1, 2, 0, 3)
    kernel_one = weight_one.reshape(32, 32, 3, 3, 3).transpose(2, 3, 0, 4, 1).reshape(288, 96)
    kernel_two = weight_two.reshape(128, 32, 3, 3, 3).transpose(4, 2, 3, 1, 0).reshape(864, 128)
    back, beyond, square = contributions(cells, kernel_two)
    def from_corner(block):
        flat = [
            (((i - 1) % grid_x) * grid_y + (j - 1) % grid_y, i * grid_y + j)
            for i in range(grid_x)
            for j in range(grid_y)
        ]
        return lax.ppermute(block, ("y", "zh", "gc", "core"), flat)

    side = from_y(beyond[0:4], -1)
    corner = from_x(back[4:6], -1) + from_corner(beyond[4:6])
    back = back[0:4] + side
    group = lax.axis_size("y") * lax.axis_size("gc")
    keep, send = sums(group, core, inner, field, outer, back, corner, cells, square, kernel_one)
    height = ROWS // group
    deep = lax.axis_size("zh")

    def exchanged(parts, axes):
        return lax.all_to_all(parts, axes, 0, 0, tiled=True)

    def narrow(parts):
        return parts.astype(jnp.float16)

    parts = small_call(
        pack_kernel, "pack", (group, 2, height, LANES), F32, keep, other_core(send[0:ROWS].astype(BF16)), other_core(send[ROWS:])
    )
    parts = exchanged(narrow(parts), ("y", "gc")).astype(F32)
    own = small_call(total_kernel, "total", (3, height, LANES), BF16, parts)
    own = jnp.stack(
        [own]
        + [lax.ppermute(own, "zh", [(i, i ^ step) for i in range(deep)]) for step in range(1, deep)]
    )
    own = small_call(
        functools.partial(deep_kernel, group), "deep", (2, height, LANES), F32, own
    )
    own = jnp.broadcast_to(narrow(own)[None], (group,) + own.shape)
    gathered = exchanged(own, ("y", "gc")).astype(F32)
    mine = updates(float(total_cells), core, gathered, plane_order())
    update_one, update_two = picked(core, mine, other_core(mine))
    return (update_one, update_two.T)


def solution(mesh):
    grid_x, grid_y = mesh.shape["gx"], mesh.shape["gy"]
    deep = max(grid_x // 4, 2)
    inner = Mesh(
        mesh.devices.reshape(grid_x // deep, deep, grid_y // 2, 2), ("y", "zh", "gc", "core")
    )
    split = P(None, ("y", "zh"), ("gc", "core"), None)
    return jax.shard_map(
        on_device,
        mesh=inner,
        in_specs=(split, P(), P(), split),
        out_specs=(P(), P()),
        check_vma=False,
    )
```

```python
import functools
import math

import jax
import jax.numpy as jnp
from jax import lax
from jax.experimental import pallas as pl
from jax.experimental.pallas import tpu as pltpu
from jax.sharding import Mesh, PartitionSpec as P

ITERS = 3
DAMPING = 0.1
F32 = jnp.float32
BF16 = jnp.bfloat16
VMEM_LIMIT = 20 * 1024 * 1024
ROWS = 1024
LANES = 128


def dot_nt(left, right):
    return lax.dot_general(left, right, (((1,), (1,)), ((), ())), preferred_element_type=F32)


def dot_nn(left, right):
    return jnp.dot(left, right, preferred_element_type=F32)


def lane_ids(shape):
    return lax.broadcasted_iota(jnp.int32, shape, 1)


def from_below(values):
    return jnp.where(lane_ids(values.shape) == 0, 0.0, pltpu.roll(values, 1, 1))


def from_above(values):
    return jnp.where(
        lane_ids(values.shape) == LANES - 1, 0.0, pltpu.roll(values, LANES - 1, 1)
    )


def contribution_kernel(cells_ref, weight_ref, rest_ref, send_ref, square_ref, acc_ref, flat_ref):
    weight = weight_ref[...]
    acc_ref[...] = jnp.zeros_like(acc_ref)
    for x in range(4):
        for y in range(2):
            place = slice((x * 2 + y) * LANES, (x * 2 + y + 1) * LANES)
            flat_ref[:, place] = cells_ref[x, y]
        terms = dot_nn(weight, flat_ref[:, x * 256 : (x + 1) * 256])
        for e in range(3):
            for a in range(3):
                for b in range(3):
                    first = (9 * e + 3 * a + b) * 32
                    lanes = slice(b * LANES, (b + 2) * LANES)
                    acc_ref[e, x + a, :, lanes] = (
                        acc_ref[e, x + a, :, lanes] + terms[first : first + 32]
                    )
    for row in range(6):
        for y in range(4):
            lanes = slice(y * LANES, (y + 1) * LANES)
            total = (
                from_above(acc_ref[0, row, :, lanes])
                + acc_ref[1, row, :, lanes]
                + from_below(acc_ref[2, row, :, lanes])
            )
            if y < 2:
                rest_ref[row, y] = total
            else:
                send_ref[row, y - 2] = total
    cells = flat_ref[...]
    square_ref[...] = dot_nt(cells, cells)


def stacked_products(left_ref, stack_ref, out_ref):
    out_ref[:, 0:864] = dot_nt(left_ref[...], stack_ref[...])
    lower = stack_ref[96:288, :]
    first = dot_nt(lower, stack_ref[288:384, :])
    second = dot_nt(lower, stack_ref[576:672, :])
    out_ref[0:96, 864:960] = first[0:96]
    out_ref[0:96, 960:1056] = first[96:192]
    out_ref[0:96, 1056:1152] = second[0:96]
    out_ref[0:96, 1152:1248] = second[96:192]
    out_ref[0:96, 1248:1280] = jnp.zeros((96, 32), F32)


def chunk_pieces(tile, group):
    used = 960 // group
    first, last = 96 * tile, 96 * tile + 96
    for chunk in range(first // used, (last - 1) // used + 1):
        low, high = max(first, chunk * used), min(last, (chunk + 1) * used)
        yield low - first, high - low, chunk, low - chunk * used


def sums_kernel(
    group, core_ref, inner_ref, own_ref, outer_ref, back_ref, corner_ref, cells_ref, square_ref, weight_ref,
    keep_ref, send_ref,
    shifted_ref, hidden_ref, acc_ref, stack_one_ref, stack_two_ref,
    rows_one_ref, rows_two_ref, out_one_ref, out_two_ref,
):
    is_first = core_ref[0] == 0
    for x in range(8):
        for y in range(6):
            if 2 <= y < 4:
                column = own_ref[x, y - 2].astype(F32)
            else:
                inner = inner_ref[x, y % 2].astype(F32)
                outer = outer_ref[x, y % 2].astype(F32)
                column = jnp.where(is_first == (y < 2), outer, inner)
            lanes = slice((x * 6 + y) * LANES, (x * 6 + y + 1) * LANES)
            shifted_ref[0:32, lanes] = from_below(column).astype(BF16)
            shifted_ref[32:64, lanes] = column.astype(BF16)
            shifted_ref[64:96, lanes] = from_above(column).astype(BF16)
    weight = weight_ref[...]
    acc_ref[...] = jnp.zeros_like(acc_ref)
    for x in range(8):
        terms = dot_nn(weight, shifted_ref[:, x * 768 : (x + 1) * 768])
        for a in range(3):
            row = x - a + 1
            if 1 <= row <= 6:
                total = acc_ref[row - 1]
                for b in range(3):
                    first = (3 * a + b) * 32
                    total = total + terms[first : first + 32, b * LANES : b * LANES + 512]
                acc_ref[row - 1] = total
    for row in range(6):
        linear = acc_ref[row]
        logistic = 1.0 / (1.0 + jnp.exp(-linear))
        hidden = (linear * logistic).astype(BF16).astype(F32)
        for y in range(4):
            column = hidden[:, y * LANES : (y + 1) * LANES]
            lanes = slice((row * 4 + y) * LANES, (row * 4 + y + 1) * LANES)
            hidden_ref[0:32, lanes] = from_below(column).astype(BF16)
            hidden_ref[32:64, lanes] = column.astype(BF16)
            hidden_ref[64:96, lanes] = from_above(column).astype(BF16)
        if row < 4:
            slope = logistic * (1.0 + linear * (1.0 - logistic))
            for y in range(2):
                back = back_ref[row, y]
                if row < 2:
                    back = back + corner_ref[row, y]
                place = slice((row * 2 + y) * LANES, (row * 2 + y + 1) * LANES)
                signal = back * slope[:, y * LANES : (y + 1) * LANES]
                rows_one_ref[96:128, place] = signal.astype(BF16)
                rows_two_ref[96:224, place] = cells_ref[row, y]
    for a in range(3):
        for b in range(3):
            rows = slice((3 * a + b) * 96, (3 * a + b + 1) * 96)
            for x in range(4):
                lanes = slice(x * 256, (x + 1) * 256)
                one = ((x + a) * 6 + b) * LANES
                two = ((x + a) * 4 + b) * LANES
                stack_one_ref[rows, lanes] = shifted_ref[:, one : one + 256]
                stack_two_ref[rows, lanes] = hidden_ref[:, two : two + 256]
    rows_one_ref[0:96, :] = stack_one_ref[0:96, :]
    rows_two_ref[0:96, :] = stack_two_ref[0:96, :]
    stacked_products(rows_one_ref, stack_one_ref, out_one_ref)
    stacked_products(rows_two_ref, stack_two_ref, out_two_ref)
    signal = rows_one_ref[96:128, :]
    square_one = dot_nt(signal, signal)

    def put(rows, one, two):
        keep_ref[rows, :] = jnp.where(is_first, one, two)
        send_ref[rows, :] = jnp.where(is_first, two, one)

    height = ROWS // group
    keep_ref[0:ROWS, :] = jnp.zeros((ROWS, LANES), F32)
    send_ref[0:ROWS, :] = jnp.zeros((ROWS, LANES), F32)
    for tile in range(10):
        lanes = slice(tile * LANES, (tile + 1) * LANES)
        for row, count, chunk, place in chunk_pieces(tile, group):
            first = chunk * height + place
            put(
                slice(first, first + count),
                out_one_ref[row : row + count, lanes],
                out_two_ref[row : row + count, lanes],
            )
    nothing = jnp.zeros((96, LANES), F32)
    for tile in range(7):
        lanes = slice(tile * LANES, (tile + 1) * LANES)
        one = out_one_ref[96:128, lanes]
        two = out_two_ref[96:224, lanes]
        if tile == 6:
            one = jnp.where(lane_ids(one.shape) < 96, one, 0.0)
            two = jnp.where(lane_ids(two.shape) < 96, two, 0.0)
        put(
            slice(ROWS + tile * 128, ROWS + (tile + 1) * 128),
            jnp.concatenate([one, nothing], axis=0),
            two,
        )
    wide = jnp.concatenate([square_one, jnp.zeros((32, 96), F32)], axis=1)
    put(
        slice(ROWS + 896, ROWS + 1024), jnp.concatenate([wide, nothing], axis=0), square_ref[...]
    )


def split_rows(values):
    high = values.astype(BF16)
    low = (values - high.astype(F32)).astype(BF16)
    return jnp.concatenate([high, low], axis=0)


LN2 = math.log(2.0)


def power_of(values):
    largest = jnp.max(jnp.max(jnp.abs(values), axis=0, keepdims=True), axis=1, keepdims=True)
    return jnp.ceil(jnp.log(jnp.maximum(largest, 1e-30)) * (1.0 / LN2)) - 14.0


def two_to(power):
    return jnp.exp(power * LN2)


def pack_kernel(keep_ref, corr_ref, grad_ref, out_ref):
    group, _, height, _ = out_ref.shape
    used = 960 // group
    plain = 896 // height
    edge = ROWS + plain * height
    for section, first, last, low, high in (
        (0, 0, ROWS, 0, group),
        (1, ROWS, edge, 0, plain),
        (1, edge, 2 * ROWS, plain, group),
    ):
        if section == 0:
            other = corr_ref[...].astype(F32)
        else:
            other = grad_ref[first - ROWS : last - ROWS, :]
        values = keep_ref[first:last, :] + other
        power = power_of(values)
        values = (values * two_to(-power)).reshape(high - low, height, LANES)
        out_ref[low:high, section] = values
        if section == 0:
            corr_power = power
        else:
            out_ref[low:high, 0, used + 1 : used + 2, :] = jnp.broadcast_to(
                power.reshape(1, 1, 1), (high - low, 1, LANES)
            )
    out_ref[:, 0, used : used + 1, :] = jnp.broadcast_to(
        corr_power.reshape(1, 1, 1), (group, 1, LANES)
    )


def opened(parts_ref, group):
    used = 960 // group
    powers = parts_ref[:, 0]
    corr = powers * two_to(powers[:, used : used + 1])
    rows = lax.broadcasted_iota(jnp.int32, corr.shape, 1)
    corr = jnp.where(rows < used, corr, 0.0)
    grad = parts_ref[:, 1] * two_to(powers[:, used + 1 : used + 2])
    return corr, grad


def total_kernel(parts_ref, out_ref):
    corr, grad = opened(parts_ref, parts_ref.shape[0])
    corr, grad = jnp.sum(corr, axis=0), jnp.sum(grad, axis=0)
    high = grad.astype(BF16)
    out_ref[0] = corr.astype(BF16)
    out_ref[1] = high
    out_ref[2] = (grad - high.astype(F32)).astype(BF16)


def deep_kernel(group, parts_ref, out_ref):
    used = 960 // group
    parts = parts_ref[...].astype(F32)
    corr = jnp.sum(parts[:, 0], axis=0)
    grad = jnp.sum(parts[:, 1] + parts[:, 2], axis=0)
    for section, values in ((0, corr), (1, grad)):
        power = power_of(values)
        out_ref[section] = values * two_to(-power)
        if section == 0:
            corr_power = power
        else:
            out_ref[0, used + 1 : used + 2, :] = jnp.broadcast_to(power, (1, LANES))
    out_ref[0, used : used + 1, :] = jnp.broadcast_to(corr_power, (1, LANES))


def small_call(kernel, name, shape, dtype, *arrays):
    return pl.pallas_call(
        kernel,
        out_shape=jax.ShapeDtypeStruct(shape, dtype),
        in_specs=in_vmem(len(arrays)),
        out_specs=in_vmem(1)[0],
        compiler_params=params(),
        name=name,
    )(*arrays)


def root_kernel(total_cells, sums_ref, out_ref, strip_ref, full_ref, factor_ref):
    group = sums_ref.shape[0]
    parts, grads = opened(sums_ref, group)
    grads = grads.reshape(ROWS, LANES)
    tiles = []
    for tile in range(10):
        pieces = [
            parts[chunk, place : place + count]
            for _, count, chunk, place in chunk_pieces(tile, group)
        ]
        tiles.append(jnp.concatenate(pieces, axis=0))
    corr = jnp.concatenate(tiles, axis=1)
    gradient = jnp.concatenate([grads[128 * j : 128 * j + 128] for j in range(7)], axis=1)[:, 0:864]

    def identity(order, dtype):
        rows = lax.broadcasted_iota(jnp.int32, (order, order), 0)
        return jnp.where(rows == lane_ids((order, order)), 1.0, 0.0).astype(dtype)

    eye_96 = identity(96, BF16)
    eye_288 = identity(288, BF16)
    strip_ref[0, :, 0:96] = dot_nt(eye_96, corr[:, 192:288].astype(BF16))
    strip_ref[0, :, 96:192] = dot_nt(eye_96, corr[:, 96:192].astype(BF16))
    strip_ref[0, :, 192:480] = corr[:, 0:288]
    strip_ref[1, :, 0:96] = corr[:, 960:1056]
    strip_ref[1, :, 96:192] = corr[:, 864:960]
    strip_ref[1, :, 192:480] = corr[:, 288:576]
    strip_ref[2, :, 0:96] = corr[:, 1152:1248]
    strip_ref[2, :, 96:192] = corr[:, 1056:1152]
    strip_ref[2, :, 192:480] = corr[:, 576:864]
    for b in range(3):
        for step in range(3):
            piece = strip_ref[step, :, (2 - b) * 96 : (2 - b) * 96 + 288]
            for a in range(3 - step):
                first = a * 288 + b * 96
                full_ref[first : first + 96, (a + step) * 288 : (a + step + 1) * 288] = piece
    turned_one = dot_nt(eye_288, full_ref[0:288, 288:576].astype(BF16))
    turned_two = dot_nt(eye_288, full_ref[0:288, 576:864].astype(BF16))
    full_ref[288:576, 0:288] = turned_one
    full_ref[576:864, 288:576] = turned_one
    full_ref[576:864, 0:288] = turned_two
    whole = full_ref[...]
    factor_ref[...] = whole.astype(BF16)
    bound = jnp.max(jnp.sum(jnp.abs(whole), axis=0, keepdims=True)) / total_cells + DAMPING
    scale = 1.0 / (bound * total_cells)
    shift = DAMPING / bound

    def times(rows):
        product = dot_nn(split_rows(rows), factor_ref[...])
        return (product[0:128] + product[128:256]) * scale + rows * shift

    def once(rows):
        return 1.5 * rows - 0.5 * times(rows)

    def iterate(rows, step):
        if step == 0:
            return once(rows)
        first = iterate(rows, step - 1)
        second = iterate(iterate(times(first), step - 1), step - 1)
        return 1.5 * first - 0.5 * second

    right = iterate(gradient, ITERS - 1)

    eye_128 = identity(128, F32)
    small = grads[896:1024] / total_cells + DAMPING * eye_128
    small_bound = jnp.max(jnp.sum(jnp.abs(small), axis=0, keepdims=True))
    scaled = small / small_bound
    root = 1.5 * eye_128 - 0.5 * scaled
    for _ in range(ITERS - 1):
        product = square_product(square_product(square_product(root, scaled), root), root)
        root = 1.5 * root - 0.5 * product
    factor = 1.0 / (math.sqrt(total_cells) * jnp.sqrt(small_bound) * jnp.sqrt(bound))
    both = split_rows(root)
    high = right.astype(BF16)
    low = (right - high.astype(F32)).astype(BF16)
    update = dot_nn(both, high)
    update = (update[0:128] + update[128:256] + dot_nn(both[0:128], low)) * factor
    update = jnp.concatenate([update, jnp.zeros((128, 32), F32)], axis=1)
    for tile in range(7):
        turned = update[:, tile * LANES : (tile + 1) * LANES].T
        for part in range(min(4, 27 - 4 * tile)):
            rows = pl.ds(4 * tile + part, 32, stride=27)
            out_ref[rows, :] = turned[part * 32 : part * 32 + 32]


def square_product(left, right):
    high = right.astype(BF16)
    low = (right - high.astype(F32)).astype(BF16)
    product = dot_nn(split_rows(left), jnp.concatenate([high, low], axis=1))
    return product[0:128, 0:128] + product[0:128, 128:256] + product[128:256, 0:128]


def pick_kernel(core_ref, mine_ref, other_ref, one_ref, two_ref):
    is_first = core_ref[0] == 0
    for tile in range(7):
        width = min(LANES, 864 - tile * LANES)
        rows = slice(tile * LANES, tile * LANES + width)
        piece = jnp.where(is_first, mine_ref[rows, :], other_ref[rows, :])
        if width < LANES:
            piece = jnp.concatenate([piece, jnp.zeros((LANES - width, LANES), F32)], axis=0)
        one_ref[:, rows] = piece.T[0:32, 0:width]
    two_ref[...] = jnp.where(is_first, other_ref[...], mine_ref[...])


def params():
    return pltpu.CompilerParams(vmem_limit_bytes=VMEM_LIMIT)


def in_vmem(count):
    return [pl.BlockSpec(memory_space=pltpu.VMEM)] * count


def contributions(cells, weight):
    shape = jax.ShapeDtypeStruct
    return pl.pallas_call(
        contribution_kernel,
        out_shape=(
            shape((6, 2, 32, LANES), F32),
            shape((6, 2, 32, LANES), F32),
            shape((128, 128), F32),
        ),
        in_specs=in_vmem(2),
        out_specs=tuple(in_vmem(3)),
        scratch_shapes=[pltpu.VMEM((3, 6, 32, 512), F32), pltpu.VMEM((128, 1024), BF16)],
        compiler_params=params(),
        cost_estimate=pl.CostEstimate(
            flops=300_000_000, bytes_accessed=2_000_000, transcendentals=0
        ),
        name="contributions",
    )(cells, weight)


def sums(group, core, left, own, right, back, corner, cells, square, weight):
    shape = jax.ShapeDtypeStruct
    return pl.pallas_call(
        functools.partial(sums_kernel, group),
        out_shape=(shape((2 * ROWS, LANES), F32), shape((2 * ROWS, LANES), F32)),
        in_specs=[pl.BlockSpec(memory_space=pltpu.SMEM)] + in_vmem(8),
        out_specs=tuple(in_vmem(2)),
        scratch_shapes=[
            pltpu.VMEM((96, 6144), BF16),
            pltpu.VMEM((96, 3072), BF16),
            pltpu.VMEM((6, 32, 512), F32),
            pltpu.VMEM((864, 1024), BF16),
            pltpu.VMEM((864, 1024), BF16),
            pltpu.VMEM((128, 1024), BF16),
            pltpu.VMEM((224, 1024), BF16),
            pltpu.VMEM((128, 1280), F32),
            pltpu.VMEM((224, 1280), F32),
        ],
        compiler_params=params(),
        cost_estimate=pl.CostEstimate(
            flops=3_000_000_000, bytes_accessed=6_000_000, transcendentals=200_000
        ),
        name="sums",
    )(core, left, own, right, back, corner, cells, square, weight)


def updates(total_cells, sums):
    return pl.pallas_call(
        functools.partial(root_kernel, total_cells),
        out_shape=jax.ShapeDtypeStruct((864, 128), F32),
        in_specs=in_vmem(1),
        out_specs=in_vmem(1)[0],
        scratch_shapes=[
            pltpu.VMEM((3, 96, 512), F32),
            pltpu.VMEM((864, 864), F32),
            pltpu.VMEM((864, 864), BF16),
        ],
        compiler_params=params(),
        cost_estimate=pl.CostEstimate(
            flops=8_000_000_000, bytes_accessed=6_000_000, transcendentals=1000
        ),
        name="updates",
    )(sums)


def picked(core, mine, other):
    shape = jax.ShapeDtypeStruct
    return pl.pallas_call(
        pick_kernel,
        out_shape=(shape((32, 864), F32), shape((864, 128), F32)),
        in_specs=[pl.BlockSpec(memory_space=pltpu.SMEM)] + in_vmem(2),
        compiler_params=params(),
        name="picked",
    )(core, mine, other)


def pairs(count, offset):
    return [(i, (i + 1 if (i - offset) % 2 == 0 else i - 1) % count) for i in range(count)]


def on_device(density, weight_one, weight_two, cotangent):
    grid_x = lax.axis_size("y") * lax.axis_size("zh")
    grid_y = lax.axis_size("gc") * lax.axis_size("core")
    total_cells = 1024 * grid_x * grid_y
    core = lax.axis_index("core").astype(jnp.int32).reshape(1)

    def from_x(block, distance):
        pairs = [((i + distance) % grid_x, i) for i in range(grid_x)]
        return lax.ppermute(block, ("y", "zh"), pairs)

    def from_y(block, distance):
        pairs = [((i + distance) % grid_y, i) for i in range(grid_y)]
        return lax.ppermute(block, ("gc", "core"), pairs)

    def other_core(block):
        return lax.ppermute(block, "core", [(0, 1), (1, 0)])

    field = density.transpose(1, 2, 0, 3)
    low, high = field[0:2], field[2:4]
    even = lax.axis_index("zh") % 2 == 0
    first = lax.ppermute(jnp.where(even, high, low), ("y", "zh"), pairs(grid_x, 0))
    second = lax.ppermute(jnp.where(even, low, high), ("y", "zh"), pairs(grid_x, 1))
    field = jnp.concatenate(
        [jnp.where(even, second, first), field, jnp.where(even, first, second)], axis=0
    )
    inner = other_core(field)
    outer = lax.ppermute(field, ("gc", "core"), pairs(grid_y, 1))
    cells = cotangent.transpose(1, 2, 0, 3)
    kernel_one = weight_one.reshape(32, 32, 3, 3, 3).transpose(2, 3, 0, 4, 1).reshape(288, 96)
    kernel_two = weight_two.reshape(128, 32, 3, 3, 3).transpose(4, 2, 3, 1, 0).reshape(864, 128)
    back, beyond, square = contributions(cells, kernel_two)
    def from_corner(block):
        flat = [
            (((i - 1) % grid_x) * grid_y + (j - 1) % grid_y, i * grid_y + j)
            for i in range(grid_x)
            for j in range(grid_y)
        ]
        return lax.ppermute(block, ("y", "zh", "gc", "core"), flat)

    side = from_y(beyond[0:4], -1)
    corner = from_x(back[4:6], -1) + from_corner(beyond[4:6])
    back = back[0:4] + side
    group = lax.axis_size("y") * lax.axis_size("gc")
    keep, send = sums(group, core, inner, field, outer, back, corner, cells, square, kernel_one)
    height = ROWS // group
    deep = lax.axis_size("zh")

    def exchanged(parts, axes):
        return lax.all_to_all(parts, axes, 0, 0, tiled=True)

    def narrow(parts):
        return parts.astype(jnp.float16)

    parts = small_call(
        pack_kernel, "pack", (group, 2, height, LANES), F32, keep, other_core(send[0:ROWS].astype(BF16)), other_core(send[ROWS:])
    )
    parts = exchanged(narrow(parts), ("y", "gc")).astype(F32)
    own = small_call(total_kernel, "total", (3, height, LANES), BF16, parts)
    own = jnp.stack(
        [own]
        + [lax.ppermute(own, "zh", [(i, i ^ step) for i in range(deep)]) for step in range(1, deep)]
    )
    own = small_call(
        functools.partial(deep_kernel, group), "deep", (2, height, LANES), F32, own
    )
    own = jnp.broadcast_to(narrow(own)[None], (group,) + own.shape)
    gathered = exchanged(own, ("y", "gc")).astype(F32)
    mine = updates(float(total_cells), gathered)
    update_one, update_two = picked(core, mine, other_core(mine))
    return (update_one, update_two.T)


def solution(mesh):
    grid_x, grid_y = mesh.shape["gx"], mesh.shape["gy"]
    deep = max(grid_x // 4, 2)
    inner = Mesh(
        mesh.devices.reshape(grid_x // deep, deep, grid_y // 2, 2), ("y", "zh", "gc", "core")
    )
    split = P(None, ("y", "zh"), ("gc", "core"), None)
    return jax.shard_map(
        on_device,
        mesh=inner,
        in_specs=(split, P(), P(), split),
        out_specs=(P(), P()),
        check_vma=False,
    )
```

```python
import functools
import math

import jax
import jax.numpy as jnp
from jax import lax
from jax.experimental import pallas as pl
from jax.experimental.pallas import tpu as pltpu
from jax.sharding import Mesh, PartitionSpec as P

ITERS = 3
DAMPING = 0.1
F32 = jnp.float32
BF16 = jnp.bfloat16
VMEM_LIMIT = 20 * 1024 * 1024
ROWS = 1024
LANES = 128


def dot_nt(left, right):
    return lax.dot_general(left, right, (((1,), (1,)), ((), ())), preferred_element_type=F32)


def dot_nn(left, right):
    return jnp.dot(left, right, preferred_element_type=F32)


def lane_ids(shape):
    return lax.broadcasted_iota(jnp.int32, shape, 1)


def from_below(values):
    return jnp.where(lane_ids(values.shape) == 0, 0.0, pltpu.roll(values, 1, 1))


def from_above(values):
    return jnp.where(
        lane_ids(values.shape) == LANES - 1, 0.0, pltpu.roll(values, LANES - 1, 1)
    )


def contribution_kernel(cells_ref, weight_ref, rest_ref, send_ref, square_ref, acc_ref, flat_ref):
    weight = weight_ref[...]
    acc_ref[...] = jnp.zeros_like(acc_ref)
    for x in range(4):
        for y in range(2):
            place = slice((x * 2 + y) * LANES, (x * 2 + y + 1) * LANES)
            flat_ref[:, place] = cells_ref[x, y]
        terms = dot_nn(weight, flat_ref[:, x * 256 : (x + 1) * 256])
        for e in range(3):
            for a in range(3):
                for b in range(3):
                    first = (9 * e + 3 * a + b) * 32
                    lanes = slice(b * LANES, (b + 2) * LANES)
                    acc_ref[e, x + a, :, lanes] = (
                        acc_ref[e, x + a, :, lanes] + terms[first : first + 32]
                    )
    for row in range(6):
        for y in range(4):
            lanes = slice(y * LANES, (y + 1) * LANES)
            total = (
                from_above(acc_ref[0, row, :, lanes])
                + acc_ref[1, row, :, lanes]
                + from_below(acc_ref[2, row, :, lanes])
            )
            if y < 2:
                rest_ref[row, y] = total
            else:
                send_ref[row, y - 2] = total
    cells = flat_ref[...]
    square_ref[...] = dot_nt(cells, cells)


def stacked_products(left_ref, stack_ref, out_ref):
    out_ref[:, 0:864] = dot_nt(left_ref[...], stack_ref[...])
    lower = stack_ref[96:288, :]
    first = dot_nt(lower, stack_ref[288:384, :])
    second = dot_nt(lower, stack_ref[576:672, :])
    out_ref[0:96, 864:960] = first[0:96]
    out_ref[0:96, 960:1056] = first[96:192]
    out_ref[0:96, 1056:1152] = second[0:96]
    out_ref[0:96, 1152:1248] = second[96:192]
    out_ref[0:96, 1248:1280] = jnp.zeros((96, 32), F32)


def chunk_pieces(tile, group):
    used = 960 // group
    first, last = 96 * tile, 96 * tile + 96
    for chunk in range(first // used, (last - 1) // used + 1):
        low, high = max(first, chunk * used), min(last, (chunk + 1) * used)
        yield low - first, high - low, chunk, low - chunk * used


def sums_kernel(
    group, core_ref, inner_ref, own_ref, outer_ref, back_ref, corner_ref, cells_ref, square_ref, weight_ref,
    keep_ref, send_ref,
    shifted_ref, hidden_ref, acc_ref, stack_one_ref, stack_two_ref,
    rows_one_ref, rows_two_ref, out_one_ref, out_two_ref, away_ref,
):
    is_first = core_ref[0] == 0
    for x in range(8):
        for y in range(6):
            if 2 <= y < 4:
                column = own_ref[x, y - 2].astype(F32)
            else:
                inner = inner_ref[x, y % 2].astype(F32)
                outer = outer_ref[x, y % 2].astype(F32)
                column = jnp.where(is_first == (y < 2), outer, inner)
            lanes = slice((x * 6 + y) * LANES, (x * 6 + y + 1) * LANES)
            shifted_ref[0:32, lanes] = from_below(column).astype(BF16)
            shifted_ref[32:64, lanes] = column.astype(BF16)
            shifted_ref[64:96, lanes] = from_above(column).astype(BF16)
    weight = weight_ref[...]
    acc_ref[...] = jnp.zeros_like(acc_ref)
    for x in range(8):
        terms = dot_nn(weight, shifted_ref[:, x * 768 : (x + 1) * 768])
        for a in range(3):
            row = x - a + 1
            if 1 <= row <= 6:
                total = acc_ref[row - 1]
                for b in range(3):
                    first = (3 * a + b) * 32
                    total = total + terms[first : first + 32, b * LANES : b * LANES + 512]
                acc_ref[row - 1] = total
    for row in range(6):
        linear = acc_ref[row]
        logistic = 1.0 / (1.0 + jnp.exp(-linear))
        hidden = (linear * logistic).astype(BF16).astype(F32)
        for y in range(4):
            column = hidden[:, y * LANES : (y + 1) * LANES]
            lanes = slice((row * 4 + y) * LANES, (row * 4 + y + 1) * LANES)
            hidden_ref[0:32, lanes] = from_below(column).astype(BF16)
            hidden_ref[32:64, lanes] = column.astype(BF16)
            hidden_ref[64:96, lanes] = from_above(column).astype(BF16)
        if row < 4:
            slope = logistic * (1.0 + linear * (1.0 - logistic))
            for y in range(2):
                back = back_ref[row, y]
                if row < 2:
                    back = back + corner_ref[row, y]
                place = slice((row * 2 + y) * LANES, (row * 2 + y + 1) * LANES)
                signal = back * slope[:, y * LANES : (y + 1) * LANES]
                rows_one_ref[96:128, place] = signal.astype(BF16)
                rows_two_ref[96:224, place] = cells_ref[row, y]
    for a in range(3):
        for b in range(3):
            rows = slice((3 * a + b) * 96, (3 * a + b + 1) * 96)
            for x in range(4):
                lanes = slice(x * 256, (x + 1) * 256)
                one = ((x + a) * 6 + b) * LANES
                two = ((x + a) * 4 + b) * LANES
                stack_one_ref[rows, lanes] = shifted_ref[:, one : one + 256]
                stack_two_ref[rows, lanes] = hidden_ref[:, two : two + 256]
    rows_one_ref[0:96, :] = stack_one_ref[0:96, :]
    rows_two_ref[0:96, :] = stack_two_ref[0:96, :]
    stacked_products(rows_one_ref, stack_one_ref, out_one_ref)
    stacked_products(rows_two_ref, stack_two_ref, out_two_ref)
    signal = rows_one_ref[96:128, :]
    square_one = dot_nt(signal, signal)

    def put(rows, one, two):
        keep_ref[rows, :] = jnp.where(is_first, one, two)
        away_ref[rows, :] = jnp.where(is_first, two, one)

    height = ROWS // group
    keep_ref[0:ROWS, :] = jnp.zeros((ROWS, LANES), F32)
    away_ref[0:ROWS, :] = jnp.zeros((ROWS, LANES), F32)
    for tile in range(10):
        lanes = slice(tile * LANES, (tile + 1) * LANES)
        for row, count, chunk, place in chunk_pieces(tile, group):
            first = chunk * height + place
            put(
                slice(first, first + count),
                out_one_ref[row : row + count, lanes],
                out_two_ref[row : row + count, lanes],
            )
    nothing = jnp.zeros((96, LANES), F32)
    for tile in range(7):
        lanes = slice(tile * LANES, (tile + 1) * LANES)
        one = out_one_ref[96:128, lanes]
        two = out_two_ref[96:224, lanes]
        if tile == 6:
            one = jnp.where(lane_ids(one.shape) < 96, one, 0.0)
            two = jnp.where(lane_ids(two.shape) < 96, two, 0.0)
        put(
            slice(ROWS + tile * 128, ROWS + (tile + 1) * 128),
            jnp.concatenate([one, nothing], axis=0),
            two,
        )
    wide = jnp.concatenate([square_one, jnp.zeros((32, 96), F32)], axis=1)
    put(
        slice(ROWS + 896, ROWS + 1024), jnp.concatenate([wide, nothing], axis=0), square_ref[...]
    )
    send_ref[0:ROWS, :] = away_ref[0:ROWS, :].astype(BF16)
    send_ref[ROWS : 3 * ROWS, :] = split_rows(away_ref[ROWS : 2 * ROWS, :])


def split_rows(values):
    high = values.astype(BF16)
    low = (values - high.astype(F32)).astype(BF16)
    return jnp.concatenate([high, low], axis=0)


LN2 = math.log(2.0)


def power_of(values):
    largest = jnp.max(jnp.max(jnp.abs(values), axis=0, keepdims=True), axis=1, keepdims=True)
    return jnp.ceil(jnp.log(jnp.maximum(largest, 1e-30)) * (1.0 / LN2)) - 14.0


def two_to(power):
    return jnp.exp(power * LN2)


def pack_kernel(keep_ref, other_ref, out_ref):
    group, _, height, _ = out_ref.shape
    used = 960 // group
    plain = 896 // height
    edge = ROWS + plain * height
    for section, first, last, low, high in (
        (0, 0, ROWS, 0, group),
        (1, ROWS, edge, 0, plain),
        (1, edge, 2 * ROWS, plain, group),
    ):
        if section == 0:
            other = other_ref[0:ROWS, :].astype(F32)
        else:
            other = other_ref[first:last, :].astype(F32)
            other = other + other_ref[first + ROWS : last + ROWS, :].astype(F32)
        values = keep_ref[first:last, :] + other
        power = power_of(values)
        values = (values * two_to(-power)).reshape(high - low, height, LANES)
        out_ref[low:high, section] = values
        if section == 0:
            corr_power = power
        else:
            out_ref[low:high, 0, used + 1 : used + 2, :] = jnp.broadcast_to(
                power.reshape(1, 1, 1), (high - low, 1, LANES)
            )
    out_ref[:, 0, used : used + 1, :] = jnp.broadcast_to(
        corr_power.reshape(1, 1, 1), (group, 1, LANES)
    )


def opened(parts_ref, group):
    used = 960 // group
    powers = parts_ref[:, 0]
    corr = powers * two_to(powers[:, used : used + 1])
    rows = lax.broadcasted_iota(jnp.int32, corr.shape, 1)
    corr = jnp.where(rows < used, corr, 0.0)
    grad = parts_ref[:, 1] * two_to(powers[:, used + 1 : used + 2])
    return corr, grad


def total_kernel(parts_ref, out_ref):
    corr, grad = opened(parts_ref, parts_ref.shape[0])
    corr, grad = jnp.sum(corr, axis=0), jnp.sum(grad, axis=0)
    high = grad.astype(BF16)
    out_ref[0] = corr.astype(BF16)
    out_ref[1] = high
    out_ref[2] = (grad - high.astype(F32)).astype(BF16)


def deep_kernel(group, *refs):
    *part_refs, out_ref = refs
    used = 960 // group
    corr, grad = 0.0, 0.0
    for part_ref in part_refs:
        corr = corr + part_ref[0].astype(F32)
        grad = grad + part_ref[1].astype(F32) + part_ref[2].astype(F32)
    for section, values in ((0, corr), (1, grad)):
        power = power_of(values)
        out_ref[section] = values * two_to(-power)
        if section == 0:
            corr_power = power
        else:
            out_ref[0, used + 1 : used + 2, :] = jnp.broadcast_to(power, (1, LANES))
    out_ref[0, used : used + 1, :] = jnp.broadcast_to(corr_power, (1, LANES))


def small_call(kernel, name, shape, dtype, *arrays):
    return pl.pallas_call(
        kernel,
        out_shape=jax.ShapeDtypeStruct(shape, dtype),
        in_specs=in_vmem(len(arrays)),
        out_specs=in_vmem(1)[0],
        compiler_params=params(),
        name=name,
    )(*arrays)


def root_kernel(total_cells, sums_ref, out_ref, strip_ref, full_ref, factor_ref):
    group = sums_ref.shape[0]
    parts, grads = opened(sums_ref, group)
    grads = grads.reshape(ROWS, LANES)
    tiles = []
    for tile in range(10):
        pieces = [
            parts[chunk, place : place + count]
            for _, count, chunk, place in chunk_pieces(tile, group)
        ]
        tiles.append(jnp.concatenate(pieces, axis=0))
    corr = jnp.concatenate(tiles, axis=1)
    gradient = jnp.concatenate([grads[128 * j : 128 * j + 128] for j in range(7)], axis=1)[:, 0:864]

    def identity(order, dtype):
        rows = lax.broadcasted_iota(jnp.int32, (order, order), 0)
        return jnp.where(rows == lane_ids((order, order)), 1.0, 0.0).astype(dtype)

    eye_96 = identity(96, BF16)
    eye_288 = identity(288, BF16)
    strip_ref[0, :, 0:96] = dot_nt(eye_96, corr[:, 192:288].astype(BF16))
    strip_ref[0, :, 96:192] = dot_nt(eye_96, corr[:, 96:192].astype(BF16))
    strip_ref[0, :, 192:480] = corr[:, 0:288]
    strip_ref[1, :, 0:96] = corr[:, 960:1056]
    strip_ref[1, :, 96:192] = corr[:, 864:960]
    strip_ref[1, :, 192:480] = corr[:, 288:576]
    strip_ref[2, :, 0:96] = corr[:, 1152:1248]
    strip_ref[2, :, 96:192] = corr[:, 1056:1152]
    strip_ref[2, :, 192:480] = corr[:, 576:864]
    for b in range(3):
        for step in range(3):
            piece = strip_ref[step, :, (2 - b) * 96 : (2 - b) * 96 + 288]
            for a in range(3 - step):
                first = a * 288 + b * 96
                full_ref[first : first + 96, (a + step) * 288 : (a + step + 1) * 288] = piece
    turned_one = dot_nt(eye_288, full_ref[0:288, 288:576].astype(BF16))
    turned_two = dot_nt(eye_288, full_ref[0:288, 576:864].astype(BF16))
    full_ref[288:576, 0:288] = turned_one
    full_ref[576:864, 288:576] = turned_one
    full_ref[576:864, 0:288] = turned_two
    whole = full_ref[...]
    factor_ref[...] = whole.astype(BF16)
    bound = jnp.max(jnp.sum(jnp.abs(whole), axis=0, keepdims=True)) / total_cells + DAMPING
    scale = 1.0 / (bound * total_cells)
    shift = DAMPING / bound

    def product(rows):
        both = dot_nn(split_rows(rows), factor_ref[...])
        return both[0:128] + both[128:256]

    def times(rows):
        return product(rows) * scale + rows * shift

    def once(rows):
        return rows * (1.5 - 0.5 * shift) - product(rows) * (0.5 * scale)

    def iterate(rows, step):
        if step == 0:
            return once(rows)
        first = iterate(rows, step - 1)
        second = iterate(iterate(times(first), step - 1), step - 1)
        return 1.5 * first - 0.5 * second

    right = iterate(gradient, ITERS - 1)

    eye_128 = identity(128, F32)
    small = grads[896:1024] / total_cells + DAMPING * eye_128
    small_bound = jnp.max(jnp.sum(jnp.abs(small), axis=0, keepdims=True))
    scaled = small / small_bound
    root = 1.5 * eye_128 - 0.5 * scaled
    for _ in range(ITERS - 1):
        product = square_product(square_product(square_product(root, scaled), root), root)
        root = 1.5 * root - 0.5 * product
    factor = 1.0 / (math.sqrt(total_cells) * jnp.sqrt(small_bound) * jnp.sqrt(bound))
    both = split_rows(root)
    high = right.astype(BF16)
    low = (right - high.astype(F32)).astype(BF16)
    update = dot_nn(both, high)
    update = (update[0:128] + update[128:256] + dot_nn(both[0:128], low)) * factor
    update = jnp.concatenate([update, jnp.zeros((128, 32), F32)], axis=1)
    for tile in range(7):
        turned = update[:, tile * LANES : (tile + 1) * LANES].T
        for part in range(min(4, 27 - 4 * tile)):
            rows = pl.ds(4 * tile + part, 32, stride=27)
            out_ref[rows, :] = turned[part * 32 : part * 32 + 32]


def square_product(left, right):
    high = right.astype(BF16)
    low = (right - high.astype(F32)).astype(BF16)
    product = dot_nn(split_rows(left), jnp.concatenate([high, low], axis=1))
    return product[0:128, 0:128] + product[0:128, 128:256] + product[128:256, 0:128]


def pick_kernel(core_ref, mine_ref, other_ref, one_ref, two_ref):
    is_first = core_ref[0] == 0
    for tile in range(7):
        width = min(LANES, 864 - tile * LANES)
        rows = slice(tile * LANES, tile * LANES + width)
        piece = jnp.where(is_first, mine_ref[rows, :], other_ref[rows, :])
        if width < LANES:
            piece = jnp.concatenate([piece, jnp.zeros((LANES - width, LANES), F32)], axis=0)
        one_ref[:, rows] = piece.T[0:32, 0:width]
    two_ref[...] = jnp.where(is_first, other_ref[...], mine_ref[...])


def params():
    return pltpu.CompilerParams(vmem_limit_bytes=VMEM_LIMIT)


def in_vmem(count):
    return [pl.BlockSpec(memory_space=pltpu.VMEM)] * count


def contributions(cells, weight):
    shape = jax.ShapeDtypeStruct
    return pl.pallas_call(
        contribution_kernel,
        out_shape=(
            shape((6, 2, 32, LANES), F32),
            shape((6, 2, 32, LANES), F32),
            shape((128, 128), F32),
        ),
        in_specs=in_vmem(2),
        out_specs=tuple(in_vmem(3)),
        scratch_shapes=[pltpu.VMEM((3, 6, 32, 512), F32), pltpu.VMEM((128, 1024), BF16)],
        compiler_params=params(),
        cost_estimate=pl.CostEstimate(
            flops=300_000_000, bytes_accessed=2_000_000, transcendentals=0
        ),
        name="contributions",
    )(cells, weight)


def sums(group, core, left, own, right, back, corner, cells, square, weight):
    shape = jax.ShapeDtypeStruct
    return pl.pallas_call(
        functools.partial(sums_kernel, group),
        out_shape=(shape((2 * ROWS, LANES), F32), shape((3 * ROWS, LANES), BF16)),
        in_specs=[pl.BlockSpec(memory_space=pltpu.SMEM)] + in_vmem(8),
        out_specs=tuple(in_vmem(2)),
        scratch_shapes=[
            pltpu.VMEM((96, 6144), BF16),
            pltpu.VMEM((96, 3072), BF16),
            pltpu.VMEM((6, 32, 512), F32),
            pltpu.VMEM((864, 1024), BF16),
            pltpu.VMEM((864, 1024), BF16),
            pltpu.VMEM((128, 1024), BF16),
            pltpu.VMEM((224, 1024), BF16),
            pltpu.VMEM((128, 1280), F32),
            pltpu.VMEM((224, 1280), F32),
            pltpu.VMEM((2 * ROWS, LANES), F32),
        ],
        compiler_params=params(),
        cost_estimate=pl.CostEstimate(
            flops=3_000_000_000, bytes_accessed=6_000_000, transcendentals=200_000
        ),
        name="sums",
    )(core, left, own, right, back, corner, cells, square, weight)


def updates(total_cells, sums):
    return pl.pallas_call(
        functools.partial(root_kernel, total_cells),
        out_shape=jax.ShapeDtypeStruct((864, 128), F32),
        in_specs=in_vmem(1),
        out_specs=in_vmem(1)[0],
        scratch_shapes=[
            pltpu.VMEM((3, 96, 512), F32),
            pltpu.VMEM((864, 864), F32),
            pltpu.VMEM((864, 864), BF16),
        ],
        compiler_params=params(),
        cost_estimate=pl.CostEstimate(
            flops=8_000_000_000, bytes_accessed=6_000_000, transcendentals=1000
        ),
        name="updates",
    )(sums)


def picked(core, mine, other):
    shape = jax.ShapeDtypeStruct
    return pl.pallas_call(
        pick_kernel,
        out_shape=(shape((32, 864), F32), shape((864, 128), F32)),
        in_specs=[pl.BlockSpec(memory_space=pltpu.SMEM)] + in_vmem(2),
        compiler_params=params(),
        name="picked",
    )(core, mine, other)


def pairs(count, offset):
    return [(i, (i + 1 if (i - offset) % 2 == 0 else i - 1) % count) for i in range(count)]


def on_device(density, weight_one, weight_two, cotangent):
    grid_x = lax.axis_size("y") * lax.axis_size("zh")
    grid_y = lax.axis_size("gc") * lax.axis_size("core")
    total_cells = 1024 * grid_x * grid_y
    core = lax.axis_index("core").astype(jnp.int32).reshape(1)

    def from_x(block, distance):
        pairs = [((i + distance) % grid_x, i) for i in range(grid_x)]
        return lax.ppermute(block, ("y", "zh"), pairs)

    def from_y(block, distance):
        pairs = [((i + distance) % grid_y, i) for i in range(grid_y)]
        return lax.ppermute(block, ("gc", "core"), pairs)

    def other_core(block):
        return lax.ppermute(block, "core", [(0, 1), (1, 0)])

    field = density.transpose(1, 2, 0, 3)
    low, high = field[0:2], field[2:4]
    even = lax.axis_index("zh") % 2 == 0
    first = lax.ppermute(jnp.where(even, high, low), ("y", "zh"), pairs(grid_x, 0))
    second = lax.ppermute(jnp.where(even, low, high), ("y", "zh"), pairs(grid_x, 1))
    field = jnp.concatenate(
        [jnp.where(even, second, first), field, jnp.where(even, first, second)], axis=0
    )
    inner = other_core(field)
    outer = lax.ppermute(field, ("gc", "core"), pairs(grid_y, 1))
    cells = cotangent.transpose(1, 2, 0, 3)
    kernel_one = weight_one.reshape(32, 32, 3, 3, 3).transpose(2, 3, 0, 4, 1).reshape(288, 96)
    kernel_two = weight_two.reshape(128, 32, 3, 3, 3).transpose(4, 2, 3, 1, 0).reshape(864, 128)
    back, beyond, square = contributions(cells, kernel_two)
    def from_corner(block):
        flat = [
            (((i - 1) % grid_x) * grid_y + (j - 1) % grid_y, i * grid_y + j)
            for i in range(grid_x)
            for j in range(grid_y)
        ]
        return lax.ppermute(block, ("y", "zh", "gc", "core"), flat)

    side = from_y(beyond[0:4], -1)
    corner = from_x(back[4:6], -1) + from_corner(beyond[4:6])
    back = back[0:4] + side
    group = lax.axis_size("y") * lax.axis_size("gc")
    keep, send = sums(group, core, inner, field, outer, back, corner, cells, square, kernel_one)
    height = ROWS // group
    deep = lax.axis_size("zh")

    def exchanged(parts, axes):
        return lax.all_to_all(parts, axes, 0, 0, tiled=True)

    def narrow(parts):
        return parts.astype(jnp.float16)

    parts = small_call(
        pack_kernel, "pack", (group, 2, height, LANES), F32, keep, other_core(send)
    )
    parts = exchanged(narrow(parts), ("y", "gc")).astype(F32)
    own = small_call(total_kernel, "total", (3, height, LANES), BF16, parts)
    others = [
        lax.ppermute(own, "zh", [(i, i ^ step) for i in range(deep)]) for step in range(1, deep)
    ]
    own = small_call(
        functools.partial(deep_kernel, group), "deep", (2, height, LANES), F32, own, *others
    )
    own = jnp.broadcast_to(narrow(own)[None], (group,) + own.shape)
    gathered = exchanged(own, ("y", "gc")).astype(F32)
    mine = updates(float(total_cells), gathered)
    update_one, update_two = picked(core, mine, other_core(mine))
    return (update_one, update_two.T)


def solution(mesh):
    grid_x, grid_y = mesh.shape["gx"], mesh.shape["gy"]
    deep = max(grid_x // 4, 2)
    inner = Mesh(
        mesh.devices.reshape(grid_x // deep, deep, grid_y // 2, 2), ("y", "zh", "gc", "core")
    )
    split = P(None, ("y", "zh"), ("gc", "core"), None)
    return jax.shard_map(
        on_device,
        mesh=inner,
        in_specs=(split, P(), P(), split),
        out_specs=(P(), P()),
        check_vma=False,
    )
```

```python
import functools
import math

import jax
import jax.numpy as jnp
from jax import lax
from jax.experimental import pallas as pl
from jax.experimental.pallas import tpu as pltpu
from jax.sharding import Mesh, PartitionSpec as P

ITERS = 3
DAMPING = 0.1
F32 = jnp.float32
BF16 = jnp.bfloat16
VMEM_LIMIT = 20 * 1024 * 1024
ROWS = 1024
LANES = 128


def dot_nt(left, right):
    return lax.dot_general(left, right, (((1,), (1,)), ((), ())), preferred_element_type=F32)


def dot_nn(left, right):
    return jnp.dot(left, right, preferred_element_type=F32)


def lane_ids(shape):
    return lax.broadcasted_iota(jnp.int32, shape, 1)


def from_below(values):
    return jnp.where(lane_ids(values.shape) == 0, 0.0, pltpu.roll(values, 1, 1))


def from_above(values):
    return jnp.where(
        lane_ids(values.shape) == LANES - 1, 0.0, pltpu.roll(values, LANES - 1, 1)
    )


def contribution_kernel(cells_ref, weight_ref, rest_ref, send_ref, square_ref, acc_ref, flat_ref):
    weight = weight_ref[...]
    acc_ref[...] = jnp.zeros_like(acc_ref)
    for x in range(4):
        for y in range(2):
            place = slice((x * 2 + y) * LANES, (x * 2 + y + 1) * LANES)
            flat_ref[:, place] = cells_ref[x, y]
        terms = dot_nn(weight, flat_ref[:, x * 256 : (x + 1) * 256])
        for e in range(3):
            for a in range(3):
                for b in range(3):
                    first = (9 * e + 3 * a + b) * 32
                    lanes = slice(b * LANES, (b + 2) * LANES)
                    acc_ref[e, x + a, :, lanes] = (
                        acc_ref[e, x + a, :, lanes] + terms[first : first + 32]
                    )
    for row in range(6):
        for y in range(4):
            lanes = slice(y * LANES, (y + 1) * LANES)
            total = (
                from_above(acc_ref[0, row, :, lanes])
                + acc_ref[1, row, :, lanes]
                + from_below(acc_ref[2, row, :, lanes])
            )
            if y < 2:
                rest_ref[row, y] = total
            else:
                send_ref[row, y - 2] = total
    cells = flat_ref[...]
    square_ref[...] = dot_nt(cells, cells)


def stacked_products(left_ref, stack_ref, out_ref):
    out_ref[:, 0:864] = dot_nt(left_ref[...], stack_ref[...])
    lower = stack_ref[96:288, :]
    first = dot_nt(lower, stack_ref[288:384, :])
    second = dot_nt(lower, stack_ref[576:672, :])
    out_ref[0:96, 864:960] = first[0:96]
    out_ref[0:96, 960:1056] = first[96:192]
    out_ref[0:96, 1056:1152] = second[0:96]
    out_ref[0:96, 1152:1248] = second[96:192]
    out_ref[0:96, 1248:1280] = jnp.zeros((96, 32), F32)


def chunk_pieces(tile, group):
    used = 960 // group
    first, last = 96 * tile, 96 * tile + 96
    for chunk in range(first // used, (last - 1) // used + 1):
        low, high = max(first, chunk * used), min(last, (chunk + 1) * used)
        yield low - first, high - low, chunk, low - chunk * used


def sums_kernel(
    group, core_ref, inner_ref, own_ref, outer_ref, back_ref, corner_ref, cells_ref, square_ref, weight_ref,
    keep_ref, send_ref,
    shifted_ref, hidden_ref, acc_ref, stack_one_ref, stack_two_ref,
    rows_one_ref, rows_two_ref, out_one_ref, out_two_ref, away_ref,
):
    is_first = core_ref[0] == 0
    for x in range(8):
        for y in range(6):
            if 2 <= y < 4:
                column = own_ref[x, y - 2].astype(F32)
            else:
                inner = inner_ref[x, y % 2].astype(F32)
                outer = outer_ref[x, y % 2].astype(F32)
                column = jnp.where(is_first == (y < 2), outer, inner)
            lanes = slice((x * 6 + y) * LANES, (x * 6 + y + 1) * LANES)
            shifted_ref[0:32, lanes] = from_below(column).astype(BF16)
            shifted_ref[32:64, lanes] = column.astype(BF16)
            shifted_ref[64:96, lanes] = from_above(column).astype(BF16)
    weight = weight_ref[...]
    acc_ref[...] = jnp.zeros_like(acc_ref)
    for x in range(8):
        terms = dot_nn(weight, shifted_ref[:, x * 768 : (x + 1) * 768])
        for a in range(3):
            row = x - a + 1
            if 1 <= row <= 6:
                total = acc_ref[row - 1]
                for b in range(3):
                    first = (3 * a + b) * 32
                    total = total + terms[first : first + 32, b * LANES : b * LANES + 512]
                acc_ref[row - 1] = total
    for row in range(6):
        linear = acc_ref[row]
        logistic = 1.0 / (1.0 + jnp.exp(-linear))
        hidden = (linear * logistic).astype(BF16).astype(F32)
        for y in range(4):
            column = hidden[:, y * LANES : (y + 1) * LANES]
            lanes = slice((row * 4 + y) * LANES, (row * 4 + y + 1) * LANES)
            hidden_ref[0:32, lanes] = from_below(column).astype(BF16)
            hidden_ref[32:64, lanes] = column.astype(BF16)
            hidden_ref[64:96, lanes] = from_above(column).astype(BF16)
        if row < 4:
            slope = logistic * (1.0 + linear * (1.0 - logistic))
            for y in range(2):
                back = back_ref[row, y]
                if row < 2:
                    back = back + corner_ref[row, y]
                place = slice((row * 2 + y) * LANES, (row * 2 + y + 1) * LANES)
                signal = back * slope[:, y * LANES : (y + 1) * LANES]
                rows_one_ref[96:128, place] = signal.astype(BF16)
                rows_two_ref[96:224, place] = cells_ref[row, y]
    for a in range(3):
        for b in range(3):
            rows = slice((3 * a + b) * 96, (3 * a + b + 1) * 96)
            for x in range(4):
                lanes = slice(x * 256, (x + 1) * 256)
                one = ((x + a) * 6 + b) * LANES
                two = ((x + a) * 4 + b) * LANES
                stack_one_ref[rows, lanes] = shifted_ref[:, one : one + 256]
                stack_two_ref[rows, lanes] = hidden_ref[:, two : two + 256]
    rows_one_ref[0:96, :] = stack_one_ref[0:96, :]
    rows_two_ref[0:96, :] = stack_two_ref[0:96, :]
    stacked_products(rows_one_ref, stack_one_ref, out_one_ref)
    stacked_products(rows_two_ref, stack_two_ref, out_two_ref)
    signal = rows_one_ref[96:128, :]
    square_one = dot_nt(signal, signal)

    def put(rows, one, two):
        keep_ref[rows, :] = jnp.where(is_first, one, two)
        away_ref[rows, :] = jnp.where(is_first, two, one)

    height = ROWS // group
    keep_ref[0:ROWS, :] = jnp.zeros((ROWS, LANES), F32)
    away_ref[0:ROWS, :] = jnp.zeros((ROWS, LANES), F32)
    for tile in range(10):
        lanes = slice(tile * LANES, (tile + 1) * LANES)
        for row, count, chunk, place in chunk_pieces(tile, group):
            first = chunk * height + place
            put(
                slice(first, first + count),
                out_one_ref[row : row + count, lanes],
                out_two_ref[row : row + count, lanes],
            )
    nothing = jnp.zeros((96, LANES), F32)
    for tile in range(7):
        lanes = slice(tile * LANES, (tile + 1) * LANES)
        one = out_one_ref[96:128, lanes]
        two = out_two_ref[96:224, lanes]
        if tile == 6:
            one = jnp.where(lane_ids(one.shape) < 96, one, 0.0)
            two = jnp.where(lane_ids(two.shape) < 96, two, 0.0)
        put(
            slice(ROWS + tile * 128, ROWS + (tile + 1) * 128),
            jnp.concatenate([one, nothing], axis=0),
            two,
        )
    wide = jnp.concatenate([square_one, jnp.zeros((32, 96), F32)], axis=1)
    put(
        slice(ROWS + 896, ROWS + 1024), jnp.concatenate([wide, nothing], axis=0), square_ref[...]
    )
    send_ref[0:ROWS, :] = away_ref[0:ROWS, :].astype(BF16)
    send_ref[ROWS : 3 * ROWS, :] = split_rows(away_ref[ROWS : 2 * ROWS, :])


def split_rows(values):
    high = values.astype(BF16)
    low = (values - high.astype(F32)).astype(BF16)
    return jnp.concatenate([high, low], axis=0)


LN2 = math.log(2.0)


def power_of(values):
    largest = jnp.max(jnp.max(jnp.abs(values), axis=0, keepdims=True), axis=1, keepdims=True)
    return jnp.ceil(jnp.log(jnp.maximum(largest, 1e-30)) * (1.0 / LN2)) - 14.0


def two_to(power):
    return jnp.exp(power * LN2)


def pack_kernel(keep_ref, other_ref, out_ref):
    group, _, height, _ = out_ref.shape
    used = 960 // group
    plain = 896 // height
    edge = ROWS + plain * height
    for section, first, last, low, high in (
        (0, 0, ROWS, 0, group),
        (1, ROWS, edge, 0, plain),
        (1, edge, 2 * ROWS, plain, group),
    ):
        if section == 0:
            other = other_ref[0:ROWS, :].astype(F32)
        else:
            other = other_ref[first:last, :].astype(F32)
            other = other + other_ref[first + ROWS : last + ROWS, :].astype(F32)
        values = keep_ref[first:last, :] + other
        power = power_of(values)
        values = (values * two_to(-power)).reshape(high - low, height, LANES)
        out_ref[low:high, section] = values
        if section == 0:
            corr_power = power
        else:
            out_ref[low:high, 0, used + 1 : used + 2, :] = jnp.broadcast_to(
                power.reshape(1, 1, 1), (high - low, 1, LANES)
            )
    out_ref[:, 0, used : used + 1, :] = jnp.broadcast_to(
        corr_power.reshape(1, 1, 1), (group, 1, LANES)
    )


def opened(parts_ref, group):
    used = 960 // group
    powers = parts_ref[:, 0]
    corr = powers * two_to(powers[:, used : used + 1])
    rows = lax.broadcasted_iota(jnp.int32, corr.shape, 1)
    corr = jnp.where(rows < used, corr, 0.0)
    grad = parts_ref[:, 1] * two_to(powers[:, used + 1 : used + 2])
    return corr, grad


def total_kernel(parts_ref, out_ref):
    corr, grad = opened(parts_ref, parts_ref.shape[0])
    corr, grad = jnp.sum(corr, axis=0), jnp.sum(grad, axis=0)
    high = grad.astype(BF16)
    out_ref[0] = corr.astype(BF16)
    out_ref[1] = high
    out_ref[2] = (grad - high.astype(F32)).astype(BF16)


def deep_kernel(group, *refs):
    *part_refs, out_ref = refs
    used = 960 // group
    corr, grad = 0.0, 0.0
    for part_ref in part_refs:
        corr = corr + part_ref[0].astype(F32)
        grad = grad + part_ref[1].astype(F32) + part_ref[2].astype(F32)
    for section, values in ((0, corr), (1, grad)):
        power = power_of(values)
        out_ref[section] = values * two_to(-power)
        if section == 0:
            corr_power = power
        else:
            out_ref[0, used + 1 : used + 2, :] = jnp.broadcast_to(power, (1, LANES))
    out_ref[0, used : used + 1, :] = jnp.broadcast_to(corr_power, (1, LANES))


def small_call(kernel, name, shape, dtype, *arrays):
    return pl.pallas_call(
        kernel,
        out_shape=jax.ShapeDtypeStruct(shape, dtype),
        in_specs=in_vmem(len(arrays)),
        out_specs=in_vmem(1)[0],
        compiler_params=params(),
        name=name,
    )(*arrays)


def root_kernel(total_cells, sums_ref, out_ref, strip_ref, full_ref, factor_ref):
    group = sums_ref.shape[0]
    parts, grads = opened(sums_ref, group)
    grads = grads.reshape(ROWS, LANES)
    tiles = []
    for tile in range(10):
        pieces = [
            parts[chunk, place : place + count]
            for _, count, chunk, place in chunk_pieces(tile, group)
        ]
        tiles.append(jnp.concatenate(pieces, axis=0))
    corr = jnp.concatenate(tiles, axis=1)
    gradient = jnp.concatenate([grads[128 * j : 128 * j + 128] for j in range(7)], axis=1)[:, 0:864]

    def identity(order, dtype):
        rows = lax.broadcasted_iota(jnp.int32, (order, order), 0)
        return jnp.where(rows == lane_ids((order, order)), 1.0, 0.0).astype(dtype)

    eye_96 = identity(96, BF16)
    eye_288 = identity(288, BF16)
    strip_ref[0, :, 0:96] = dot_nt(eye_96, corr[:, 192:288].astype(BF16))
    strip_ref[0, :, 96:192] = dot_nt(eye_96, corr[:, 96:192].astype(BF16))
    strip_ref[0, :, 192:480] = corr[:, 0:288]
    strip_ref[1, :, 0:96] = corr[:, 960:1056]
    strip_ref[1, :, 96:192] = corr[:, 864:960]
    strip_ref[1, :, 192:480] = corr[:, 288:576]
    strip_ref[2, :, 0:96] = corr[:, 1152:1248]
    strip_ref[2, :, 96:192] = corr[:, 1056:1152]
    strip_ref[2, :, 192:480] = corr[:, 576:864]
    for b in range(3):
        for step in range(3):
            piece = strip_ref[step, :, (2 - b) * 96 : (2 - b) * 96 + 288]
            for a in range(3 - step):
                first = a * 288 + b * 96
                full_ref[first : first + 96, (a + step) * 288 : (a + step + 1) * 288] = piece
    turned_one = dot_nt(eye_288, full_ref[0:288, 288:576].astype(BF16))
    turned_two = dot_nt(eye_288, full_ref[0:288, 576:864].astype(BF16))
    full_ref[288:576, 0:288] = turned_one
    full_ref[576:864, 288:576] = turned_one
    full_ref[576:864, 0:288] = turned_two
    whole = full_ref[...]
    factor_ref[...] = whole.astype(BF16)
    bound = jnp.max(jnp.sum(jnp.abs(whole), axis=0, keepdims=True)) / total_cells + DAMPING
    scale = 1.0 / (bound * total_cells)
    shift = DAMPING / bound

    def product(rows):
        both = dot_nn(split_rows(rows), factor_ref[...])
        return both[0:128] + both[128:256]

    def times(rows):
        return product(rows) * scale + rows * shift

    def once(rows):
        return rows * (1.5 - 0.5 * shift) - product(rows) * (0.5 * scale)

    def iterate(rows, step):
        if step == 0:
            return once(rows)
        first = iterate(rows, step - 1)
        second = iterate(iterate(times(first), step - 1), step - 1)
        return 1.5 * first - 0.5 * second

    right = iterate(gradient, ITERS - 1)

    eye_128 = identity(128, F32)
    small = grads[896:1024] / total_cells + DAMPING * eye_128
    small_bound = jnp.max(jnp.sum(jnp.abs(small), axis=0, keepdims=True))
    scaled = small / small_bound
    root = 1.5 * eye_128 - 0.5 * scaled
    for _ in range(ITERS - 1):
        product = square_product(square_product(square_product(root, scaled), root), root)
        root = 1.5 * root - 0.5 * product
    factor = 1.0 / (math.sqrt(total_cells) * jnp.sqrt(small_bound) * jnp.sqrt(bound))
    both = split_rows(root)
    high = right.astype(BF16)
    low = (right - high.astype(F32)).astype(BF16)
    update = dot_nn(both, high)
    update = (update[0:128] + update[128:256] + dot_nn(both[0:128], low)) * factor
    update = jnp.concatenate([update, jnp.zeros((128, 32), F32)], axis=1)
    for tile in range(7):
        turned = update[:, tile * LANES : (tile + 1) * LANES].T
        for part in range(min(4, 27 - 4 * tile)):
            rows = pl.ds(4 * tile + part, 32, stride=27)
            out_ref[rows, :] = turned[part * 32 : part * 32 + 32]


def square_product(left, right):
    high = right.astype(BF16)
    low = (right - high.astype(F32)).astype(BF16)
    product = dot_nn(split_rows(left), jnp.concatenate([high, low], axis=1))
    return product[0:128, 0:128] + product[0:128, 128:256] + product[128:256, 0:128]


def pick_kernel(core_ref, mine_ref, other_ref, one_ref, two_ref):
    is_first = core_ref[0] == 0
    for tile in range(7):
        width = min(LANES, 864 - tile * LANES)
        rows = slice(tile * LANES, tile * LANES + width)
        piece = jnp.where(is_first, mine_ref[rows, :], other_ref[rows, :])
        if width < LANES:
            piece = jnp.concatenate([piece, jnp.zeros((LANES - width, LANES), F32)], axis=0)
        one_ref[:, rows] = piece.T[0:32, 0:width]
    two_ref[...] = jnp.where(is_first, other_ref[...], mine_ref[...])


def params():
    return pltpu.CompilerParams(vmem_limit_bytes=VMEM_LIMIT)


def in_vmem(count):
    return [pl.BlockSpec(memory_space=pltpu.VMEM)] * count


def contributions(cells, weight):
    shape = jax.ShapeDtypeStruct
    return pl.pallas_call(
        contribution_kernel,
        out_shape=(
            shape((6, 2, 32, LANES), F32),
            shape((6, 2, 32, LANES), F32),
            shape((128, 128), F32),
        ),
        in_specs=in_vmem(2),
        out_specs=tuple(in_vmem(3)),
        scratch_shapes=[pltpu.VMEM((3, 6, 32, 512), F32), pltpu.VMEM((128, 1024), BF16)],
        compiler_params=params(),
        cost_estimate=pl.CostEstimate(
            flops=300_000_000, bytes_accessed=2_000_000, transcendentals=0
        ),
        name="contributions",
    )(cells, weight)


def sums(group, core, left, own, right, back, corner, cells, square, weight):
    shape = jax.ShapeDtypeStruct
    return pl.pallas_call(
        functools.partial(sums_kernel, group),
        out_shape=(shape((2 * ROWS, LANES), F32), shape((3 * ROWS, LANES), BF16)),
        in_specs=[pl.BlockSpec(memory_space=pltpu.SMEM)] + in_vmem(8),
        out_specs=tuple(in_vmem(2)),
        scratch_shapes=[
            pltpu.VMEM((96, 6144), BF16),
            pltpu.VMEM((96, 3072), BF16),
            pltpu.VMEM((6, 32, 512), F32),
            pltpu.VMEM((864, 1024), BF16),
            pltpu.VMEM((864, 1024), BF16),
            pltpu.VMEM((128, 1024), BF16),
            pltpu.VMEM((224, 1024), BF16),
            pltpu.VMEM((128, 1280), F32),
            pltpu.VMEM((224, 1280), F32),
            pltpu.VMEM((2 * ROWS, LANES), F32),
        ],
        compiler_params=params(),
        cost_estimate=pl.CostEstimate(
            flops=3_000_000_000, bytes_accessed=6_000_000, transcendentals=200_000
        ),
        name="sums",
    )(core, left, own, right, back, corner, cells, square, weight)


def updates(total_cells, sums):
    return pl.pallas_call(
        functools.partial(root_kernel, total_cells),
        out_shape=jax.ShapeDtypeStruct((864, 128), F32),
        in_specs=in_vmem(1),
        out_specs=in_vmem(1)[0],
        scratch_shapes=[
            pltpu.VMEM((3, 96, 512), F32),
            pltpu.VMEM((864, 864), F32),
            pltpu.VMEM((864, 864), BF16),
        ],
        compiler_params=params(),
        cost_estimate=pl.CostEstimate(
            flops=8_000_000_000, bytes_accessed=6_000_000, transcendentals=1000
        ),
        name="updates",
    )(sums)


def picked(core, mine, other):
    shape = jax.ShapeDtypeStruct
    return pl.pallas_call(
        pick_kernel,
        out_shape=(shape((32, 864), F32), shape((864, 128), F32)),
        in_specs=[pl.BlockSpec(memory_space=pltpu.SMEM)] + in_vmem(2),
        compiler_params=params(),
        name="picked",
    )(core, mine, other)


def pairs(count, offset):
    return [(i, (i + 1 if (i - offset) % 2 == 0 else i - 1) % count) for i in range(count)]


def on_device(density, weight_one, weight_two, cotangent):
    grid_x = lax.axis_size("y") * lax.axis_size("zh")
    grid_y = lax.axis_size("gc") * lax.axis_size("core")
    total_cells = 1024 * grid_x * grid_y
    core = lax.axis_index("core").astype(jnp.int32).reshape(1)

    def from_x(block, distance):
        pairs = [((i + distance) % grid_x, i) for i in range(grid_x)]
        return lax.ppermute(block, ("y", "zh"), pairs)

    def from_y(block, distance):
        pairs = [((i + distance) % grid_y, i) for i in range(grid_y)]
        return lax.ppermute(block, ("gc", "core"), pairs)

    def other_core(block):
        return lax.ppermute(block, "core", [(0, 1), (1, 0)])

    even = lax.axis_index("zh") % 2 == 0
    sent = jnp.where(even, density[:, 2:4], density[:, 0:2]).transpose(1, 2, 0, 3)
    sent, density = lax.optimization_barrier((sent, density))
    first = lax.ppermute(sent, ("y", "zh"), pairs(grid_x, 0))
    field = density.transpose(1, 2, 0, 3)
    low, high = field[0:2], field[2:4]
    second = lax.ppermute(jnp.where(even, low, high), ("y", "zh"), pairs(grid_x, 1))
    field = jnp.concatenate(
        [jnp.where(even, second, first), field, jnp.where(even, first, second)], axis=0
    )
    inner = other_core(field)
    outer = lax.ppermute(field, ("gc", "core"), pairs(grid_y, 1))
    cells = cotangent.transpose(1, 2, 0, 3)
    kernel_one = weight_one.reshape(32, 32, 3, 3, 3).transpose(2, 3, 0, 4, 1).reshape(288, 96)
    kernel_two = weight_two.reshape(128, 32, 3, 3, 3).transpose(4, 2, 3, 1, 0).reshape(864, 128)
    back, beyond, square = contributions(cells, kernel_two)
    def from_corner(block):
        flat = [
            (((i - 1) % grid_x) * grid_y + (j - 1) % grid_y, i * grid_y + j)
            for i in range(grid_x)
            for j in range(grid_y)
        ]
        return lax.ppermute(block, ("y", "zh", "gc", "core"), flat)

    side = from_y(beyond[0:4], -1)
    corner = from_x(back[4:6], -1) + from_corner(beyond[4:6])
    back = back[0:4] + side
    group = lax.axis_size("y") * lax.axis_size("gc")
    keep, send = sums(group, core, inner, field, outer, back, corner, cells, square, kernel_one)
    height = ROWS // group
    deep = lax.axis_size("zh")

    def exchanged(parts, axes):
        return lax.all_to_all(parts, axes, 0, 0, tiled=True)

    def narrow(parts):
        return parts.astype(jnp.float16)

    parts = small_call(
        pack_kernel, "pack", (group, 2, height, LANES), F32, keep, other_core(send)
    )
    parts = exchanged(narrow(parts), ("y", "gc")).astype(F32)
    own = small_call(total_kernel, "total", (3, height, LANES), BF16, parts)
    others = [
        lax.ppermute(own, "zh", [(i, i ^ step) for i in range(deep)]) for step in range(1, deep)
    ]
    own = small_call(
        functools.partial(deep_kernel, group), "deep", (2, height, LANES), F32, own, *others
    )
    own = jnp.broadcast_to(narrow(own)[None], (group,) + own.shape)
    gathered = exchanged(own, ("y", "gc")).astype(F32)
    mine = updates(float(total_cells), gathered)
    update_one, update_two = picked(core, mine, other_core(mine))
    return (update_one, update_two.T)


def solution(mesh):
    grid_x, grid_y = mesh.shape["gx"], mesh.shape["gy"]
    deep = max(grid_x // 4, 2)
    inner = Mesh(
        mesh.devices.reshape(grid_x // deep, deep, grid_y // 2, 2), ("y", "zh", "gc", "core")
    )
    split = P(None, ("y", "zh"), ("gc", "core"), None)
    return jax.shard_map(
        on_device,
        mesh=inner,
        in_specs=(split, P(), P(), split),
        out_specs=(P(), P()),
        check_vma=False,
    )
```
